32 devices in a mesh: parts: 2 (over y), leaf: 8 (over z, x), sub: 2 (over core).
Axes of the slice: x: 2, y: 2, z: 4, core: 2. Of those that a mesh axis runs over, the one named last changes fastest.
Arguments:
- vectors: float32 [16, 65536], P(None, ('parts', 'leaf', 'sub')), parts along dimension 1, may hold values from -6 to 6
- basis: float32 [1024, 32, 64], P(('parts', 'leaf', 'sub')), parts along dimension 0, may hold values from -0.75 to 0.75
- trans: float32 [32, 31, 2, 32, 32], P(('parts', 'leaf', 'sub')), parts along dimension 0, may hold values from -0.875 to 0.875
- upper_trans: float32 [30, 2, 32, 32], P('parts'), parts along dimension 0, may hold values from -0.875 to 0.875
- upper_coup: float32 [60, 32, 32], P('parts'), parts along dimension 0, may hold values from -1 to 1
- send_node: int32 [32, 16, 4], P(('parts', 'leaf', 'sub')), parts along dimension 0, may hold values from 0 to 62, as said below
- send_count: int32 [32, 16], P(('parts', 'leaf', 'sub')), parts along dimension 0, may hold values from 1 to 4, as said below
- coup_tgt: int32 [32, 16, 4], P(('parts', 'leaf', 'sub')), parts along dimension 0, may hold values from 0 to 62, as said below
- coup_mat: float32 [32, 16, 4, 32, 32], P(('parts', 'leaf', 'sub')), parts along dimension 0, may hold values from -1 to 1
- near_src: int32 [1024, 9], P(('parts', 'leaf', 'sub')), parts along dimension 0, may hold values from 0 to 511, as said below
- near_count: int32 [1024], P(('parts', 'leaf', 'sub')), parts along dimension 0, may hold values from 1 to 9
- near_mat: float32 [1024, 9, 64, 64], P(('parts', 'leaf', 'sub')), parts along dimension 0, may hold values from -0.75 to 0.75
Outputs:
- product: float32 [16, 65536], P(None, ('parts', 'leaf', 'sub')), parts along dimension 1
The draws below stay inside these ranges and needn't reach their ends.
There are 2 independent parts, one for each index of `parts`. The reference program is written for one: setup_inputs(seed, part) draws one part's arguments, and reference() takes and returns one part's arrays. A program takes and returns all parts, laid end to end along the dimension named above; each array names one. Nothing has to cross between parts.
Inputs may be any that keep to these rules, and one draw needn't show every extreme that they name: `send_node`: entry [s, t, j] is a node number of branch s, on the same tree level as node coup_tgt[t, s, j] of branch t. `send_count`: in every draw some branch receives 4 live slots from every branch. `coup_tgt`: A node number of branch t. near_src[l, i] differs from l by at most 16.
All inputs are finite; a program needn't handle non-finite values.
Results may differ from the reference program's by a relative error of at most 0.0003.
Values sent between devices are 32-bit elements; how exact they have to be, the bound alone decides.
No kernel may reach another device: no remote copies, remote signals or barrier semaphores. Data moves between devices by JAX's collectives and lax.ppermute only.
A program may use at most 128 MiB of HBM per device.

```python
import jax
import jax.numpy as jnp
from jax import lax

LEAF = 64
RANK = 32
NVEC = 16
NNEAR = 9
CAP = 4
LEAF_DEV = 32
GROUP = 16
LEAVES = 512
NPTS = 32768
HALO = 16


def level_table(key):
    key = jax.random.fold_in(key, 11)
    return jax.random.randint(key, (GROUP, GROUP, CAP), 0, LEAF_DEV.bit_length())


def node_of(key, levels):
    widths = jnp.right_shift(jnp.full(levels.shape, LEAF_DEV, jnp.int32), levels.astype(jnp.int32))
    picks = jax.random.randint(key, levels.shape, 0, 1 << 20) % widths
    return 2 * LEAF_DEV - 2 * widths + picks


def draw_send_node(key, part):
    levels = level_table(key)
    key = jax.random.fold_in(key, 21)
    return node_of(key, levels).astype(jnp.int32)


def draw_coup_tgt(key, part):
    levels = level_table(key)
    key = jax.random.fold_in(key, 22)
    return node_of(key, jnp.transpose(levels, (1, 0, 2))).astype(jnp.int32)


def draw_send_count(key, part):
    key = jax.random.fold_in(key, 31)
    first, second, third = jax.random.split(key, 3)
    base = jax.random.randint(first, (GROUP, GROUP), 1, 4)
    heavy = (jax.random.randint(second, (GROUP,), 0, 4) == 0).astype(jnp.int32)
    counts = jnp.minimum(CAP, base + 2 * heavy[None, :])
    chosen = jax.random.randint(third, (), 0, GROUP)
    columns = jnp.arange(GROUP, dtype=jnp.int32)[None, :] + jnp.zeros((GROUP, 1), jnp.int32)
    counts = jnp.where(columns == chosen, CAP, counts)
    return counts.astype(jnp.int32)


def draw_near_src(key, part):
    key = jax.random.fold_in(key, 41)
    offsets = jax.random.randint(key, (LEAVES, NNEAR), -HALO, HALO + 1)
    rows = jnp.arange(LEAVES, dtype=jnp.int32)[:, None]
    slots = jnp.arange(NNEAR, dtype=jnp.int32)[None, :]
    edges = jnp.where(rows % 2 == 0, HALO, -HALO)
    offsets = jnp.where(slots == 0, 0, jnp.where(slots == 1, edges, offsets))
    return jnp.clip(rows + offsets, 0, LEAVES - 1).astype(jnp.int32)


def draw_near_count(key, part):
    key = jax.random.fold_in(key, 51)
    first, second, third = jax.random.split(key, 3)
    dense = jnp.repeat(jax.random.randint(first, (GROUP,), 0, 2), LEAF_DEV)
    higher = jax.random.randint(second, (LEAVES,), max(1, NNEAR - 2), NNEAR + 1)
    lower = jax.random.randint(third, (LEAVES,), 1, min(NNEAR, 3) + 1)
    counts = jnp.where(dense == 1, higher, lower)
    counts = jnp.where(jnp.arange(LEAVES, dtype=jnp.int32) % LEAF_DEV == 0, NNEAR, counts)
    return counts.astype(jnp.int32)


def steps_of(rng, extent, shards, low, largest):
    level = 1.0
    for dim, parts in shards:
        heights = jax.random.uniform(jax.random.fold_in(jax.random.fold_in(rng, 6), dim), (parts,), jnp.float32, low / len(shards), largest / len(shards))
        level = level * jnp.repeat(jnp.exp(heights), extent[dim] // parts).reshape((-1,) + (1,) * (len(extent) - 1 - dim))
    return level


def scatter_about(rng, dims, width, limit, cuts=(), held_as=jnp.bfloat16):
    entries = jax.random.normal(rng, dims, jnp.float32) * width
    if len(cuts) > 0:
        entries = steps_of(rng, dims, cuts, -0.22, 0.18) * entries
    return jnp.clip(entries, min=-limit, max=limit).astype(held_as)


def setup_inputs(seed: int = 0, part: int = 0) -> dict:
    keys = jax.random.split(jax.random.key(seed), 13)
    part_keys = jax.random.split(jax.random.fold_in(keys[12], part), 13)
    return {
        "vectors": scatter_about(part_keys[0], (NVEC, NPTS), 1.0, 6.0, ((1, 16),), jnp.float32),
        "basis": scatter_about(part_keys[1], (LEAVES, RANK, LEAF), LEAF ** -0.5, 0.75, ((0, 16),), jnp.float32),
        "trans": scatter_about(part_keys[2], (GROUP, LEAF_DEV - 1, 2, RANK, RANK), (RANK * 3 // 2) ** -0.5, 0.875, ((0, 16),), jnp.float32),
        "upper_trans": scatter_about(part_keys[3], (GROUP - 1, 2, RANK, RANK), (RANK * 3 // 2) ** -0.5, 0.875, (), jnp.float32),
        "upper_coup": scatter_about(part_keys[4], (2 * GROUP - 2, RANK, RANK), RANK ** -0.5, 1.0, (), jnp.float32),
        "send_node": draw_send_node(jax.random.fold_in(jax.random.fold_in(keys[12], part), 71), part),
        "send_count": draw_send_count(jax.random.fold_in(jax.random.fold_in(keys[12], part), 71), part),
        "coup_tgt": draw_coup_tgt(jax.random.fold_in(jax.random.fold_in(keys[12], part), 71), part),
        "coup_mat": scatter_about(part_keys[8], (GROUP, GROUP, CAP, RANK, RANK), RANK ** -0.5, 1.0, ((0, 16),), jnp.float32),
        "near_src": draw_near_src(jax.random.fold_in(jax.random.fold_in(keys[12], part), 71), part),
        "near_count": draw_near_count(jax.random.fold_in(jax.random.fold_in(keys[12], part), 71), part),
        "near_mat": scatter_about(part_keys[11], (LEAVES, NNEAR, LEAF, LEAF), LEAF ** -0.5, 0.75, ((0, 16),), jnp.float32),
    }


def contract(formula, first, second):
    return jnp.einsum(formula, first, second, precision=lax.Precision.HIGHEST)


def upper_tree(tops, upper_trans, upper_coup):
    members = tops.shape[0]
    height = members.bit_length() - 1
    rank_size = tops.shape[1]
    vec_size = tops.shape[2]
    layers = [tops]
    for j in range(1, height):
        number = members >> j
        offset = members - (members >> (j - 1))
        children = layers[-1].reshape(number, 2, rank_size, vec_size)
        layers.append(contract("ncab,ncbv->nav", upper_trans[offset:offset + number], children))
    couplings = []
    for j in range(height):
        number = members >> j
        sibling = layers[j].reshape(number // 2, 2, rank_size, vec_size)[:, ::-1].reshape(number, rank_size, vec_size)
        offset = 2 * members - 2 * number
        couplings.append(contract("nab,nbv->nav", upper_coup[offset:offset + number], sibling))
    result = couplings[height - 1]
    for j in range(height - 1, 0, -1):
        number = members >> j
        offset = members - (members >> (j - 1))
        spread = contract("ncab,nav->ncbv", upper_trans[offset:offset + number], result)
        result = couplings[j - 1] + spread.reshape(2 * number, rank_size, vec_size)
    return result


def local_up(leaf_coef, trans):
    layers = [leaf_coef]
    offset = 0
    number = leaf_coef.shape[-3] // 2
    while number >= 1:
        last = layers[-1]
        children = last.reshape(last.shape[:-3] + (number, 2) + last.shape[-2:])
        layers.append(contract("...ncab,...ncbv->...nav", trans[..., offset:offset + number, :, :, :], children))
        offset = offset + number
        number = number // 2
    return jnp.concatenate(layers, axis=-3)


def local_down(node_terms, trans):
    nodes = node_terms.shape[-3]
    leaves = (nodes + 1) // 2
    number = 1
    result = node_terms[..., nodes - 1:nodes, :, :]
    while number < leaves:
        toffset = leaves - 2 * number
        spread = contract("...ncab,...nav->...ncbv", trans[..., toffset:toffset + number, :, :, :], result)
        doubled = 2 * number
        noffset = 2 * leaves - 2 * doubled
        result = node_terms[..., noffset:noffset + doubled, :, :] + spread.reshape(spread.shape[:-4] + (doubled,) + spread.shape[-2:])
        number = doubled
    return result


def reference(vectors, basis, trans, upper_trans, upper_coup, send_node, send_count, coup_tgt, coup_mat, near_src, near_count, near_mat):
    leaf_values = vectors.reshape(NVEC, LEAVES, LEAF)
    leaf_coef = contract("lrp,vlp->lrv", basis, leaf_values).reshape(GROUP, LEAF_DEV, RANK, NVEC)
    nodes_all = local_up(leaf_coef, trans)
    top_term = upper_tree(nodes_all[:, -1], upper_trans, upper_coup)
    slot_ids = jnp.arange(CAP, dtype=jnp.int32)
    sources = jnp.arange(GROUP, dtype=jnp.int32)

    def receive(items):
        target, matrices, targets = items
        picked = nodes_all[sources[:, None], send_node[:, target, :]]
        live = (slot_ids[None, :] < send_count[:, target][:, None]).astype(jnp.float32)
        picked = picked * live[:, :, None, None]
        pieces = contract("scab,scbv->scav", matrices, picked)
        empty = jnp.zeros((2 * LEAF_DEV - 1, RANK, NVEC), jnp.float32)
        return empty.at[targets.reshape(-1)].add(pieces.reshape(GROUP * CAP, RANK, NVEC))

    far_terms = lax.map(receive, (sources, coup_mat, coup_tgt))
    far_terms = far_terms.at[:, -1].add(top_term)
    leaf_terms = local_down(far_terms, trans).reshape(LEAVES, RANK, NVEC)
    far_part = contract("lrp,lrv->vlp", basis, leaf_terms)
    live_near = (jnp.arange(NNEAR, dtype=jnp.int32)[None, :] < near_count[:, None]).astype(jnp.float32)
    neighbours = leaf_values[:, near_src] * live_near[None, :, :, None]
    near_part = contract("lnpq,vlnq->vlp", near_mat, neighbours)
    return (far_part + near_part).reshape(NVEC, LEAVES * LEAF)
```

```python
import functools

import jax
import jax.numpy as jnp
from jax import lax
from jax.experimental import pallas as pl
from jax.experimental.pallas import tpu as pltpu
from jax.sharding import PartitionSpec as P

BRANCH = ("leaf", "sub")
LANES = 128
F32 = jnp.float32
BF16 = jnp.bfloat16
MIB = 1 << 20


def split(x):
    high = x.astype(BF16)
    low = (x - high.astype(F32)).astype(BF16)
    return high, low


def contract_nt(a, b):
    return lax.dot_general(a, b, (((1,), (1,)), ((), ())), preferred_element_type=F32)


def contract_nn(a, b):
    return lax.dot_general(a, b, (((1,), (0,)), ((), ())), preferred_element_type=F32)


def contract_tn(a, b):
    return lax.dot_general(a, b, (((0,), (0,)), ((), ())), preferred_element_type=F32)


def times(x, high, low, dot):
    rows = x.shape[0]
    x_high, x_low = split(x)
    both = dot(jnp.concatenate([x_high, x_low], axis=0), high)
    return both[:rows] + both[rows:] + dot(x_high, low)


def product(a, b, dot):
    a_high, a_low = split(a)
    b_high, b_low = split(b)
    return dot(a_high, b_high) + (dot(a_high, b_low) + dot(a_low, b_high))


def lane_part(rows, part):
    return lax.broadcasted_iota(jnp.int32, (rows, LANES), 1) // part


def over(count, body, step=16):
    if count <= step:
        for i in range(count):
            body(i)
    else:

        def several(k, carry):
            for u in range(step):
                body(k * step + u)
            return carry

        lax.fori_loop(0, count // step, several, 0)


def fetch(sources, targets, semaphores):
    copies = []
    for i, (source, target) in enumerate(zip(sources, targets)):
        copies.append(pltpu.make_async_copy(source, target, semaphores.at[i]))
        copies[i].start()
    return copies


def up_kernel(
    members,
    slots,
    vec_far,
    basis_far,
    trans_far,
    send_node_far,
    send_count_far,
    outgoing,
    sub_half,
    cross_half,
    weights,
    vec,
    basis,
    trans,
    send_node,
    send_count,
    rolled,
    semaphores,
):
    arriving = fetch(
        (vec_far, basis_far, trans_far, send_node_far, send_count_far),
        (vec, basis, trans, send_node, send_count),
        semaphores,
    )
    basis_high, basis_low, trans_high, trans_low = (weights.at[i] for i in range(4))
    position = lax.axis_index(BRANCH)
    leaf_dev, rank, leaf_size = basis.shape
    vecs = vec.shape[0]
    arriving[0].wait()
    arriving[1].wait()
    half = vec.shape[1] // 2
    even = position % 2 == 0
    low_half = vec[:, :half]
    high_half = vec[:, half:]
    sub_half[...] = jnp.where(even, high_half, low_half)
    cross_half[...] = jnp.where(even, low_half, high_half)

    for leaf in range(leaf_dev):
        group, q = leaf // 4, leaf % 4
        blank = jnp.zeros((rank, LANES - leaf_size), F32)
        pieces = [basis[leaf], blank] if q % 2 == 0 else [blank, basis[leaf]]
        high, low = split(jnp.concatenate(pieces, axis=1))
        rows = slice(q * rank, (q + 1) * rank)
        here = slice(0, LANES) if q < 2 else slice(LANES, 2 * LANES)
        other = slice(LANES, 2 * LANES) if q < 2 else slice(0, LANES)
        basis_high[group, rows, here] = high
        basis_low[group, rows, here] = low
        basis_high[group, rows, other] = jnp.zeros((rank, LANES), BF16)
        basis_low[group, rows, other] = jnp.zeros((rank, LANES), BF16)
    arriving[2].wait()
    for node in range(leaf_dev):
        group, q = node // 4, node % 4
        rows = slice(q * rank, (q + 1) * rank)
        here = slice(0, LANES) if q < 2 else slice(LANES, 2 * LANES)
        other = slice(LANES, 2 * LANES) if q < 2 else slice(0, LANES)
        if node < leaf_dev - 1:
            pair = [trans[2 * node], trans[2 * node + 1]]
            blank = jnp.zeros((rank, LANES - 2 * rank), F32)
            pieces = pair + [blank] if q % 2 == 0 else [blank] + pair
            high, low = split(jnp.concatenate(pieces, axis=1))
        else:
            high = low = jnp.zeros((rank, LANES), BF16)
        trans_high[group, rows, here] = high
        trans_low[group, rows, here] = low
        trans_high[group, rows, other] = jnp.zeros((rank, LANES), BF16)
        trans_low[group, rows, other] = jnp.zeros((rank, LANES), BF16)

    def keep(group, value):
        for k in range(4):
            rolled[4 * group + k] = value if k == 0 else pltpu.roll(value, k * rank, 1)

    level = []
    for g in range(leaf_dev // 4):
        x = vec[:, 2 * LANES * g : 2 * LANES * (g + 1)]
        level.append(times(x, basis_high[g], basis_low[g], contract_nt))
        keep(g, level[g])
    done = leaf_dev // 4
    weight = 0
    while len(level) > 1:
        nodes = []
        for g in range(len(level) // 2):
            children = jnp.concatenate([level[2 * g], level[2 * g + 1]], axis=1)
            nodes.append(times(children, trans_high[weight], trans_low[weight], contract_nt))
            keep(done, nodes[g])
            weight += 1
            done += 1
        level = nodes
    two = times(level[0], trans_high[weight, :, :LANES], trans_low[weight, :, :LANES], contract_nt)
    top = times(two, trans_high[weight, :, LANES:], trans_low[weight, :, LANES:], contract_nt)
    keep(done, two + top)
    blank_index = 4 * (done + 1)
    rolled[blank_index] = jnp.zeros((vecs, LANES), F32)

    arriving[3].wait()
    arriving[4].wait()
    part = lane_part(vecs, rank)
    few = lane_part(vecs // 2, rank)
    first = position & 3
    second = (position + 1) & 3
    top_rows = jnp.where(
        few == first,
        rolled[4 * done + ((first - 2) & 3), : vecs // 2],
        jnp.where(few == second, rolled[4 * done + ((second - 2) & 3), vecs // 2 :], 0.0),
    )

    def pick(target):
        count = send_count[0, target]
        value = None
        for j in range(slots):
            node = send_node[j, target]
            index = (node >> 2) * 4 + ((j - node) & 3)
            piece = rolled[jnp.where(j < count, index, blank_index)]
            value = piece if value is None else jnp.where(part == j, piece, value)
        outgoing[target, :vecs] = value
        outgoing[target, vecs:] = top_rows

    over(members, pick)


def prepare_kernel(
    members,
    slots,
    coup_mat_far,
    upper_trans_far,
    upper_coup_far,
    far_high,
    far_low,
    coup_mat,
    upper_trans,
    upper_coup,
    semaphores,
):
    arriving = fetch(
        (coup_mat_far, upper_trans_far, upper_coup_far), (coup_mat, upper_trans, upper_coup), semaphores
    )
    position = lax.axis_index(BRANCH)
    for copy in arriving:
        copy.wait()
    rank = coup_mat.shape[1]
    height = members.bit_length() - 1

    def one(source):
        for j in range(slots):
            block = coup_mat[source * slots + j]
            pieces = []
            if j > 0:
                pieces.append(jnp.zeros((rank, j * rank), F32))
            pieces.append(block)
            if j < slots - 1:
                pieces.append(jnp.zeros((rank, (slots - 1 - j) * rank), F32))
            high, low = split(jnp.concatenate(pieces, axis=1))
            far_high[source, j * rank : (j + 1) * rank] = high
            far_low[source, j * rank : (j + 1) * rank] = low

    over(members, one)

    nothing = jnp.zeros((members // 4, LANES, LANES), BF16)
    far_high[members:] = nothing
    far_low[members:] = nothing
    blank = jnp.zeros((rank, LANES - rank), F32)

    def place(group, value):
        high, low = split(value)
        far_high[members + group, 2 * rank : 3 * rank] = high
        far_low[members + group, 2 * rank : 3 * rank] = low

    own = jnp.zeros((rank, LANES), F32)
    path = None
    for j in range(height):
        number = members >> j
        node = position >> j
        if j > 0:
            mixer = members - (members >> (j - 1)) + node
            step = upper_trans[mixer * 2 + ((position >> (j - 1)) & 1)]
            path = step if path is None else product(step, path, contract_nn)
        coupler = upper_coup[2 * members - 2 * number + node]
        start = coupler if path is None else product(path, coupler, contract_tn)
        current = [(node ^ 1, start)]
        for lower in range(j, 0, -1):
            offset = members - (members >> (lower - 1))
            following = []
            for index, matrix in current:
                for c in range(2):
                    mixed = product(matrix, upper_trans[(offset + index) * 2 + c], contract_nn)
                    following.append((2 * index + c, mixed))
            current = following
        if j < 2:
            for index, matrix in current:
                wide = jnp.concatenate([matrix, blank], axis=1)
                own = own + pltpu.roll(wide, (index & 3) * rank, 1)
        else:
            for k in range(0, len(current), 4):
                wide = jnp.concatenate([matrix for _, matrix in current[k : k + 4]], axis=1)
                place(current[k][0] >> 2, wide)
    place(position >> 2, own)


def near_kernel(
    vec_far,
    sub_half,
    cross_half,
    near_mat_far,
    near_src_far,
    near_count_far,
    near,
    vec,
    near_mat,
    near_src,
    near_count,
    values,
    semaphores,
    block_semaphores,
):
    arriving = fetch((vec_far, near_src_far, near_count_far), (vec, near_src, near_count), semaphores)
    chunks = block_semaphores.shape[0]
    chunk = near_mat.shape[0] // chunks

    def chunk_copy(k):
        rows = pl.ds(k * chunk, chunk)
        return pltpu.make_async_copy(near_mat_far.at[rows], near_mat.at[rows], block_semaphores.at[k])

    for k in range(chunks):
        chunk_copy(k).start()
    position = lax.axis_index(BRANCH)
    for copy in arriving:
        copy.wait()
    leaf_dev, slots, leaf_size, _ = near_mat.shape
    vecs = vec.shape[0]
    even = position % 2 == 0
    halo = leaf_dev // 2
    left = lane_part(vecs, leaf_size) == 0

    def lay(base, block):
        for m in range(block.shape[1] // LANES):
            pair = block[:, m * LANES : (m + 1) * LANES]
            swapped = pltpu.roll(pair, leaf_size, 1)
            for c, twice in enumerate((jnp.where(left, pair, swapped), jnp.where(left, swapped, pair))):
                high, low = split(twice)
                values[base + 2 * m + c, :vecs] = high
                values[base + 2 * m + c, vecs:] = low

    lay(halo, vec[...])
    lay(0, jnp.where(even, cross_half[...], sub_half[...]))
    lay(halo + leaf_dev, jnp.where(even, sub_half[...], cross_half[...]))
    values[2 * leaf_dev] = jnp.zeros((2 * vecs, LANES), BF16)
    shift = halo - position * leaf_dev
    wide_left = lane_part(2 * vecs, leaf_size) == 0
    out_left = lane_part(vecs, leaf_size) == 0

    def source(leaf, slot):
        live = slot < near_count[0, leaf]
        return values[jnp.where(live, near_src[slot, leaf] + shift, 2 * leaf_dev)]

    def two_leaves(pair):
        total = None
        leaves = (2 * pair, 2 * pair + 1)
        for tile in range(0, slots, 4):
            columns = min(4, slots - tile)
            rows_x = []
            rows_w = []
            for leaf in leaves:
                xs = []
                ws = []
                for i in range(tile, tile + columns, 2):
                    if i + 1 < tile + columns:
                        xs.append(jnp.where(wide_left, source(leaf, i), source(leaf, i + 1)))
                        ws.append(jnp.concatenate([near_mat[leaf, i], near_mat[leaf, i + 1]], axis=1))
                    else:
                        xs.append(source(leaf, i))
                        blank = jnp.zeros((leaf_size, LANES - leaf_size), F32)
                        ws.append(jnp.concatenate([near_mat[leaf, i], blank], axis=1))
                rows_x.append(jnp.concatenate(xs, axis=1) if len(xs) > 1 else xs[0])
                rows_w.append(jnp.concatenate(ws, axis=1) if len(ws) > 1 else ws[0])
            x = jnp.concatenate(rows_x, axis=0)
            high, low = split(jnp.concatenate(rows_w, axis=0))
            term = contract_nt(x, high) + contract_nt(x, low)
            total = term if total is None else total + term
        first = total[:vecs] + total[vecs : 2 * vecs]
        second = total[2 * vecs : 3 * vecs] + total[3 * vecs :]
        lanes = pl.ds(pl.multiple_of(pair * LANES, LANES), LANES)
        near[:, lanes] = jnp.where(out_left, first, second)

    def body(k, carry):
        chunk_copy(k).wait()
        for m in range(chunk // 2):
            two_leaves(k * (chunk // 2) + m)
        return carry

    lax.fori_loop(0, chunks, body, 0)


def down_kernel(
    members,
    slots,
    incoming,
    far_high,
    far_low,
    weights,
    near,
    coup_tgt_far,
    out,
    coup_tgt,
    far,
    semaphores,
):
    arriving = fetch((coup_tgt_far,), (coup_tgt,), semaphores)
    basis_high, basis_low, trans_high, trans_low = (weights.at[i] for i in range(4))
    vecs = out.shape[0]
    rank = LANES // slots
    groups = far.shape[0]
    far[...] = jnp.zeros(far.shape, F32)
    part = lane_part(vecs, rank)
    arriving[0].wait()

    def scatter(source):
        piece = times(incoming[source, :vecs], far_high[source], far_low[source], contract_nt)
        for j in range(slots):
            node = coup_tgt[j, source]
            alone = jnp.where(part == j, piece, 0.0)
            far[node >> 2] += pltpu.roll(alone, ((node - j) & 3) * rank, 1)

    over(members, scatter)

    few = lane_part(vecs // 2, rank)
    term = jnp.zeros((vecs, LANES), F32)
    for g in range(members // 4):
        first = jnp.zeros((vecs // 2, LANES), F32)
        second = jnp.zeros((vecs // 2, LANES), F32)
        for q in range(4):
            rows = incoming[4 * g + q, vecs:]
            first = jnp.where(few == q, rows, first)
            second = jnp.where(few == (q + 1) % 4, rows, second)
        tops = jnp.concatenate([first, pltpu.roll(second, LANES - rank, 1)], axis=0)
        term = term + times(tops, far_high[members + g], far_low[members + g], contract_nt)

    last = groups - 1
    weight = trans_high.shape[0] - 1
    base = far[last] + term
    two = base + times(base, trans_high[weight, :, LANES:], trans_low[weight, :, LANES:], contract_nn)
    first = last - 1
    level = [far[first] + times(two, trans_high[weight, :, :LANES], trans_low[weight, :, :LANES], contract_nn)]
    while first > 0:
        first -= 2 * len(level)
        weight -= len(level)
        children = []
        for g, value in enumerate(level):
            spread = times(value, trans_high[weight + g], trans_low[weight + g], contract_nn)
            children.append(far[first + 2 * g] + spread[:, :LANES])
            children.append(far[first + 2 * g + 1] + spread[:, LANES:])
        level = children
    for g, value in enumerate(level):
        lanes = slice(2 * LANES * g, 2 * LANES * (g + 1))
        out[:, lanes] = near[:, lanes] + times(value, basis_high[g], basis_low[g], contract_nn)


def in_hbm(x):
    return pltpu.with_memory_space_constraint(x, pltpu.HBM)


HBM_SPEC = pl.BlockSpec(memory_space=pltpu.HBM)
VMEM_SPEC = pl.BlockSpec(memory_space=pltpu.VMEM)


def params(mib):
    return pltpu.CompilerParams(vmem_limit_bytes=mib * MIB)


def cost(flops, size):
    return pl.CostEstimate(flops=flops, bytes_accessed=size, transcendentals=0)


def body(
    vectors,
    basis,
    trans,
    upper_trans,
    upper_coup,
    send_node,
    send_count,
    coup_tgt,
    coup_mat,
    near_src,
    near_count,
    near_mat,
):
    vecs, points = vectors.shape
    leaf_dev, rank, leaf_size = basis.shape
    members = lax.axis_size(BRANCH)
    slots = send_node.shape[2]
    groups = leaf_dev // 4
    node_groups = 2 * groups
    trans_blocks = trans.reshape(-1, rank, rank)
    coup_blocks = coup_mat.reshape(-1, rank, rank)
    upper_blocks = upper_trans.reshape(-1, rank, rank)
    near_chunks = leaf_dev // 4
    shape = jax.ShapeDtypeStruct

    def held(*dims):
        return shape(dims, BF16)

    outgoing, sub_half, cross_half, weights = pl.pallas_call(
        functools.partial(up_kernel, members, slots),
        out_shape=[
            shape((members, vecs + vecs // 2, LANES), F32),
            shape((vecs, points // 2), F32),
            shape((vecs, points // 2), F32),
            held(4, groups, LANES, 2 * LANES),
        ],
        in_specs=[HBM_SPEC] * 5,
        out_specs=[VMEM_SPEC] * 4,
        scratch_shapes=[
            pltpu.VMEM((vecs, points), F32),
            pltpu.VMEM(basis.shape, F32),
            pltpu.VMEM(trans_blocks.shape, F32),
            pltpu.SMEM((slots, members), jnp.int32),
            pltpu.SMEM((1, members), jnp.int32),
            pltpu.VMEM((4 * node_groups + 8, vecs, LANES), F32),
            pltpu.SemaphoreType.DMA((5,)),
        ],
        compiler_params=params(8 + members // 4),
        name="up",
    )(
        in_hbm(vectors),
        in_hbm(basis),
        in_hbm(trans_blocks),
        in_hbm(jnp.transpose(send_node[0])),
        in_hbm(send_count),
    )
    incoming = lax.all_to_all(outgoing, BRANCH, split_axis=0, concat_axis=0, tiled=True)
    pairs = [(i, i ^ 1) for i in range(members)]
    sub_got = lax.ppermute(sub_half, BRANCH, pairs)
    pairs = [(i, i + 1) for i in range(1, members - 1, 2)]
    pairs = pairs + [(b, a) for a, b in pairs]
    cross_got = lax.ppermute(cross_half, BRANCH, pairs)

    far_high, far_low = pl.pallas_call(
        functools.partial(prepare_kernel, members, slots),
        out_shape=[
            held(members + members // 4, LANES, LANES),
            held(members + members // 4, LANES, LANES),
        ],
        in_specs=[HBM_SPEC] * 3,
        out_specs=[VMEM_SPEC] * 2,
        scratch_shapes=[
            pltpu.VMEM(coup_blocks.shape, F32),
            pltpu.VMEM(upper_blocks.shape, F32),
            pltpu.VMEM(upper_coup.shape, F32),
            pltpu.SemaphoreType.DMA((3,)),
        ],
        compiler_params=params(8 + members // 4),
        cost_estimate=cost(1 << 20, 4 << 20),
        name="prepare",
    )(
        in_hbm(coup_blocks),
        in_hbm(upper_blocks),
        in_hbm(upper_coup),
    )

    near = pl.pallas_call(
        near_kernel,
        out_shape=shape((vecs, points), F32),
        in_specs=[HBM_SPEC, VMEM_SPEC, VMEM_SPEC, HBM_SPEC, HBM_SPEC, HBM_SPEC],
        out_specs=VMEM_SPEC,
        scratch_shapes=[
            pltpu.VMEM((vecs, points), F32),
            pltpu.VMEM(near_mat.shape, F32),
            pltpu.SMEM(near_src.shape[::-1], jnp.int32),
            pltpu.SMEM((1, leaf_dev), jnp.int32),
            pltpu.VMEM((2 * leaf_dev + 1, 2 * vecs, LANES), BF16),
            pltpu.SemaphoreType.DMA((3,)),
            pltpu.SemaphoreType.DMA((near_chunks,)),
        ],
        compiler_params=params(16),
        cost_estimate=cost(1 << 28, 10 << 20),
        name="near",
    )(
        in_hbm(vectors),
        sub_got,
        cross_got,
        in_hbm(near_mat),
        in_hbm(jnp.transpose(near_src)),
        in_hbm(near_count.reshape(1, -1)),
    )

    return pl.pallas_call(
        functools.partial(down_kernel, members, slots),
        out_shape=shape((vecs, points), F32),
        in_specs=[VMEM_SPEC] * 5 + [HBM_SPEC],
        out_specs=VMEM_SPEC,
        scratch_shapes=[
            pltpu.SMEM((slots, members), jnp.int32),
            pltpu.VMEM((node_groups, vecs, LANES), F32),
            pltpu.SemaphoreType.DMA((1,)),
        ],
        compiler_params=params(8 + members // 4),
        name="down",
    )(
        incoming,
        far_high,
        far_low,
        weights,
        near,
        in_hbm(jnp.transpose(coup_tgt[0])),
    )


def solution(mesh):
    spread = ("parts",) + BRANCH
    return jax.shard_map(
        body,
        mesh=mesh,
        in_specs=(
            P(None, spread),
            P(spread, None, None),
            P(spread, None, None, None, None),
            P("parts", None, None, None),
            P("parts", None, None),
            P(spread, None, None),
            P(spread, None),
            P(spread, None, None),
            P(spread, None, None, None, None),
            P(spread, None),
            P(spread),
            P(spread, None, None, None),
        ),
        out_specs=P(None, spread),
        check_vma=False,
    )
```

```python
import functools

import jax
import jax.numpy as jnp
from jax import lax
from jax.experimental import pallas as pl
from jax.experimental.pallas import tpu as pltpu
from jax.sharding import PartitionSpec as P

BRANCH = ("leaf", "sub")
LANES = 128
F32 = jnp.float32
BF16 = jnp.bfloat16
MIB = 1 << 20


def split(x):
    high = x.astype(BF16)
    low = (x - high.astype(F32)).astype(BF16)
    return high, low


def contract_nt(a, b):
    return lax.dot_general(a, b, (((1,), (1,)), ((), ())), preferred_element_type=F32)


def contract_nn(a, b):
    return lax.dot_general(a, b, (((1,), (0,)), ((), ())), preferred_element_type=F32)


def contract_tn(a, b):
    return lax.dot_general(a, b, (((0,), (0,)), ((), ())), preferred_element_type=F32)


def times(x, high, low, dot):
    rows = x.shape[0]
    x_high, x_low = split(x)
    both = dot(jnp.concatenate([x_high, x_low], axis=0), high)
    return both[:rows] + both[rows:] + dot(x_high, low)


def product(a, b, dot):
    a_high, a_low = split(a)
    b_high, b_low = split(b)
    return dot(a_high, b_high) + (dot(a_high, b_low) + dot(a_low, b_high))


def lane_part(rows, part):
    return lax.broadcasted_iota(jnp.int32, (rows, LANES), 1) // part


def over(count, body, step=16):
    if count <= step:
        for i in range(count):
            body(i)
    else:

        def several(k, carry):
            for u in range(step):
                body(k * step + u)
            return carry

        lax.fori_loop(0, count // step, several, 0)


def fetch(sources, targets, semaphores):
    copies = []
    for i, (source, target) in enumerate(zip(sources, targets)):
        copies.append(pltpu.make_async_copy(source, target, semaphores.at[i]))
        copies[i].start()
    return copies


def up_kernel(
    members,
    slots,
    vec_far,
    basis_far,
    trans_far,
    send_node_far,
    send_count_far,
    outgoing,
    sub_half,
    cross_half,
    weights,
    vec,
    basis,
    trans,
    send_node,
    send_count,
    rolled,
    semaphores,
):
    position = lax.axis_index(BRANCH)
    half = vec.shape[1] // 2
    start = (position & 1) * half
    at_partner = vec_far.at[:, pl.ds(pl.multiple_of(half - start, LANES), half)]
    at_neighbour = vec_far.at[:, pl.ds(pl.multiple_of(start, LANES), half)]
    arriving = fetch(
        (vec_far, basis_far, trans_far, send_node_far, send_count_far, at_partner, at_neighbour),
        (vec, basis, trans, send_node, send_count, sub_half, cross_half),
        semaphores,
    )
    basis_high, basis_low, trans_high, trans_low = (weights.at[i] for i in range(4))
    leaf_dev, rank, leaf_size = basis.shape
    vecs = vec.shape[0]
    left = lane_part(vecs, LANES // 2) == 0
    blank = jnp.zeros((rank, LANES // 2), F32)

    arriving[0].wait()
    arriving[1].wait()
    for leaf in range(leaf_dev):
        group, q = leaf // 4, leaf % 4
        high, low = split(jnp.concatenate([basis[leaf], blank] if q % 2 == 0 else [blank, basis[leaf]], axis=1))
        basis_high[group, q * rank : (q + 1) * rank] = high
        basis_low[group, q * rank : (q + 1) * rank] = low
    def keep(group, value):
        for k in range(4):
            rolled[4 * group + k] = value if k == 0 else pltpu.roll(value, k * rank, 1)

    def joined(first, second, high, low):
        both = times(jnp.concatenate([first, second], axis=0), high, low, contract_nt)
        return jnp.where(left, both[:vecs], both[vecs:])

    level = []
    for g in range(leaf_dev // 4):
        first = vec[:, 2 * LANES * g : 2 * LANES * g + LANES]
        second = vec[:, 2 * LANES * g + LANES : 2 * LANES * (g + 1)]
        level.append(joined(first, second, basis_high[g], basis_low[g]))
        keep(g, level[g])
    arriving[2].wait()
    for node in range(leaf_dev):
        group, q = node // 4, node % 4
        if node < leaf_dev - 1:
            pair = [trans[2 * node], trans[2 * node + 1]]
            high, low = split(jnp.concatenate(pair + [blank] if q % 2 == 0 else [blank] + pair, axis=1))
        else:
            high = low = jnp.zeros((rank, LANES), BF16)
        trans_high[group, q * rank : (q + 1) * rank] = high
        trans_low[group, q * rank : (q + 1) * rank] = low
    done = leaf_dev // 4
    weight = 0
    while len(level) > 1:
        nodes = []
        for g in range(len(level) // 2):
            nodes.append(joined(level[2 * g], level[2 * g + 1], trans_high[weight], trans_low[weight]))
            keep(done, nodes[g])
            weight += 1
            done += 1
        level = nodes
    two = jnp.where(left, times(level[0], trans_high[weight], trans_low[weight], contract_nt), 0.0)
    top = times(two, trans_high[weight], trans_low[weight], contract_nt)
    keep(done, jnp.where(left, two, top))
    blank_index = 4 * (done + 1)
    rolled[blank_index] = jnp.zeros((vecs, LANES), F32)

    arriving[3].wait()
    arriving[4].wait()
    part = lane_part(vecs, rank)
    few = lane_part(vecs // 2, rank)
    first = position & 3
    second = (position + 1) & 3
    top_rows = jnp.where(
        few == first,
        rolled[4 * done + ((first - 2) & 3), : vecs // 2],
        jnp.where(few == second, rolled[4 * done + ((second - 2) & 3), vecs // 2 :], 0.0),
    )

    def pick(target):
        count = send_count[0, target]
        value = None
        for j in range(slots):
            node = send_node[j, target]
            index = (node >> 2) * 4 + ((j - node) & 3)
            piece = rolled[jnp.where(j < count, index, blank_index)]
            value = piece if value is None else jnp.where(part == j, piece, value)
        outgoing[target, :vecs] = value
        outgoing[target, vecs:] = top_rows

    over(members, pick)
    arriving[5].wait()
    arriving[6].wait()


def prepare(members, slots, coup_mat, upper_trans, upper_coup, far_high, far_low):
    position = lax.axis_index(BRANCH)
    rank = coup_mat.shape[1]
    height = members.bit_length() - 1

    def one(source):
        for j in range(slots):
            pieces = [coup_mat[source * slots + j]]
            if j > 0:
                pieces.insert(0, jnp.zeros((rank, j * rank), F32))
            if j < slots - 1:
                pieces.append(jnp.zeros((rank, (slots - 1 - j) * rank), F32))
            high, low = split(jnp.concatenate(pieces, axis=1))
            far_high[source, j * rank : (j + 1) * rank] = high
            far_low[source, j * rank : (j + 1) * rank] = low

    over(members, one)

    nothing = jnp.zeros((members // 4, LANES, LANES), BF16)
    far_high[members:] = nothing
    far_low[members:] = nothing
    blank = jnp.zeros((rank, LANES - rank), F32)

    def place(group, value):
        high, low = split(value)
        far_high[members + group, 2 * rank : 3 * rank] = high
        far_low[members + group, 2 * rank : 3 * rank] = low

    own = jnp.zeros((rank, LANES), F32)
    path = None
    for j in range(height):
        number = members >> j
        node = position >> j
        if j > 0:
            mixer = members - (members >> (j - 1)) + node
            step = upper_trans[mixer * 2 + ((position >> (j - 1)) & 1)]
            path = step if path is None else product(step, path, contract_nn)
        coupler = upper_coup[2 * members - 2 * number + node]
        start = coupler if path is None else product(path, coupler, contract_tn)
        current = [(node ^ 1, start)]
        for lower in range(j, 0, -1):
            offset = members - (members >> (lower - 1))
            following = []
            for index, matrix in current:
                for c in range(2):
                    mixed = product(matrix, upper_trans[(offset + index) * 2 + c], contract_nn)
                    following.append((2 * index + c, mixed))
            current = following
        if j < 2:
            for index, matrix in current:
                wide = jnp.concatenate([matrix, blank], axis=1)
                own = own + pltpu.roll(wide, (index & 3) * rank, 1)
        else:
            for k in range(0, len(current), 4):
                wide = jnp.concatenate([matrix for _, matrix in current[k : k + 4]], axis=1)
                place(current[k][0] >> 2, wide)
    place(position >> 2, own)


def near_half(
    first,
    halo_half,
    vec_far,
    near_src_far,
    near_count_far,
    near_mat_far,
    near,
    vec,
    near_src,
    near_count,
    near_mat,
    values,
    semaphores,
    block_semaphores,
    before,
):
    position = lax.axis_index(BRANCH)
    leaves, near_slots, leaf_size, _ = near_mat.shape
    leaf_dev = 2 * leaves
    vecs = vec.shape[0]
    halo = leaf_dev // 2
    upper = (position & 1) ^ (1 if first else 0)
    base = upper * leaves
    arriving = fetch((vec_far, near_src_far, near_count_far), (vec, near_src, near_count), semaphores)
    chunks = block_semaphores.shape[0]
    chunk = leaves // chunks

    def chunk_copy(k):
        here = pl.ds(k * chunk, chunk)
        return pltpu.make_async_copy(
            near_mat_far.at[pl.ds(base + k * chunk, chunk)], near_mat.at[here], block_semaphores.at[k]
        )

    for k in range(chunks):
        chunk_copy(k).start()
    before()
    for copy in arriving:
        copy.wait()
    left = lane_part(vecs, leaf_size) == 0

    def lay(base, block):
        for m in range(block.shape[1] // LANES):
            pair = block[:, m * LANES : (m + 1) * LANES]
            swapped = pltpu.roll(pair, leaf_size, 1)
            for c, twice in enumerate((jnp.where(left, pair, swapped), jnp.where(left, swapped, pair))):
                high, low = split(twice)
                values[base + 2 * m + c, :vecs] = high
                values[base + 2 * m + c, vecs:] = low

    lay(upper * (halo + leaf_dev), halo_half[...])
    lay(halo, vec[...])
    values[2 * leaf_dev] = jnp.zeros((2 * vecs, LANES), BF16)
    shift = halo - position * leaf_dev
    wide_left = lane_part(2 * vecs, leaf_size) == 0

    def source(leaf, slot):
        live = slot < near_count[0, base + leaf]
        return values[jnp.where(live, near_src[slot, base + leaf] + shift, 2 * leaf_dev)]

    def two_leaves(pair):
        total = None
        leaves = (2 * pair, 2 * pair + 1)
        for tile in range(0, near_slots, 4):
            columns = min(4, near_slots - tile)
            rows_x = []
            rows_w = []
            for leaf in leaves:
                xs = []
                ws = []
                for i in range(tile, tile + columns, 2):
                    if i + 1 < tile + columns:
                        xs.append(jnp.where(wide_left, source(leaf, i), source(leaf, i + 1)))
                        ws.append(jnp.concatenate([near_mat[leaf, i], near_mat[leaf, i + 1]], axis=1))
                    else:
                        xs.append(source(leaf, i))
                        blank = jnp.zeros((leaf_size, LANES - leaf_size), F32)
                        ws.append(jnp.concatenate([near_mat[leaf, i], blank], axis=1))
                rows_x.append(jnp.concatenate(xs, axis=1) if len(xs) > 1 else xs[0])
                rows_w.append(jnp.concatenate(ws, axis=1) if len(ws) > 1 else ws[0])
            x = jnp.concatenate(rows_x, axis=0)
            high, low = split(jnp.concatenate(rows_w, axis=0))
            term = contract_nt(x, high) + contract_nt(x, low)
            total = term if total is None else total + term
        first = total[:vecs] + total[vecs : 2 * vecs]
        second = total[2 * vecs : 3 * vecs] + total[3 * vecs :]
        lanes = pl.ds(pl.multiple_of((base // 2 + pair) * LANES, LANES), LANES)
        near[:, lanes] = jnp.where(left, first, second)

    for k in range(chunks):
        chunk_copy(k).wait()
        for m in range(chunk // 2):
            two_leaves(k * (chunk // 2) + m)


def first_kernel(
    members,
    slots,
    halo_half,
    vec_far,
    near_src_far,
    near_count_far,
    near_mat_far,
    coup_mat_far,
    upper_trans_far,
    upper_coup_far,
    near,
    far_high,
    far_low,
    coup_mat,
    upper_trans,
    upper_coup,
    prepare_semaphores,
    *scratch,
):
    arriving = fetch(
        (upper_trans_far, upper_coup_far, coup_mat_far), (upper_trans, upper_coup, coup_mat), prepare_semaphores
    )

    def before():
        for copy in arriving:
            copy.wait()
        prepare(members, slots, coup_mat, upper_trans, upper_coup, far_high, far_low)

    near_half(True, halo_half, vec_far, near_src_far, near_count_far, near_mat_far, near, *scratch, before)


def second_kernel(halo_half, vec_far, near_src_far, near_count_far, near_mat_far, near_first, near, *scratch):
    del near_first
    near_half(
        False, halo_half, vec_far, near_src_far, near_count_far, near_mat_far, near, *scratch, lambda: None
    )


def down_kernel(
    members,
    slots,
    incoming,
    far_high,
    far_low,
    weights,
    near,
    coup_tgt_far,
    out,
    coup_tgt,
    far,
    pieces,
    semaphores,
):
    arriving = fetch((coup_tgt_far,), (coup_tgt,), semaphores)
    basis_high, basis_low, trans_high, trans_low = (weights.at[i] for i in range(4))
    vecs = out.shape[0]
    rank = LANES // slots
    groups = far.shape[0]
    far[...] = jnp.zeros(far.shape, F32)
    part = lane_part(vecs, rank)

    def couple(source):
        pieces[source] = times(incoming[source, :vecs], far_high[source], far_low[source], contract_nt)

    over(members, couple)

    few = lane_part(vecs // 2, rank)
    term = jnp.zeros((vecs, LANES), F32)
    for g in range(members // 4):
        first = jnp.zeros((vecs // 2, LANES), F32)
        second = jnp.zeros((vecs // 2, LANES), F32)
        for q in range(4):
            rows = incoming[4 * g + q, vecs:]
            first = jnp.where(few == q, rows, first)
            second = jnp.where(few == (q + 1) % 4, rows, second)
        tops = jnp.concatenate([first, pltpu.roll(second, LANES - rank, 1)], axis=0)
        term = term + times(tops, far_high[members + g], far_low[members + g], contract_nt)
    arriving[0].wait()

    def scatter(source):
        piece = pieces[source]
        for j in range(slots):
            node = coup_tgt[j, source]
            alone = jnp.where(part == j, piece, 0.0)
            far[node >> 2] += pltpu.roll(alone, ((node - j) & 3) * rank, 1)

    over(members, scatter)

    left = part < 2
    weight = trans_high.shape[0] - 1

    def first_half(x):
        return jnp.where(left, x, 0.0)

    def second_half(x):
        return jnp.where(left, 0.0, x)

    def spread(x, high, low):
        both = times(jnp.concatenate([first_half(x), second_half(x)], axis=0), high, low, contract_nn)
        return both[:vecs], both[vecs:]

    first = groups - 2
    high, low = trans_high[weight], trans_low[weight]
    base = far[first + 1] + term
    two = base + times(second_half(base), high, low, contract_nn)
    level = [far[first] + times(first_half(two), high, low, contract_nn)]
    while first > 0:
        first -= 2 * len(level)
        weight -= len(level)
        children = []
        for g, value in enumerate(level):
            pair = spread(value, trans_high[weight + g], trans_low[weight + g])
            children.append(far[first + 2 * g] + pair[0])
            children.append(far[first + 2 * g + 1] + pair[1])
        level = children
    for g, value in enumerate(level):
        for c, points in enumerate(spread(value, basis_high[g], basis_low[g])):
            lanes = slice(LANES * (2 * g + c), LANES * (2 * g + c + 1))
            out[:, lanes] = near[:, lanes] + points


def in_hbm(x):
    return pltpu.with_memory_space_constraint(x, pltpu.HBM)


HBM_SPEC = pl.BlockSpec(memory_space=pltpu.HBM)
VMEM_SPEC = pl.BlockSpec(memory_space=pltpu.VMEM)


def params(mib):
    return pltpu.CompilerParams(vmem_limit_bytes=mib * MIB)


def cost(flops, size):
    return pl.CostEstimate(flops=flops, bytes_accessed=size, transcendentals=0)


def body(
    vectors,
    basis,
    trans,
    upper_trans,
    upper_coup,
    send_node,
    send_count,
    coup_tgt,
    coup_mat,
    near_src,
    near_count,
    near_mat,
):
    vecs, points = vectors.shape
    leaf_dev, rank, leaf_size = basis.shape
    members = lax.axis_size(BRANCH)
    slots = send_node.shape[2]
    groups = leaf_dev // 4
    node_groups = 2 * groups
    trans_blocks = trans.reshape(-1, rank, rank)
    coup_blocks = coup_mat.reshape(-1, rank, rank)
    upper_blocks = upper_trans.reshape(-1, rank, rank)
    near_chunks = leaf_dev // 16
    shape = jax.ShapeDtypeStruct

    def held(*dims):
        return shape(dims, BF16)

    outgoing, sub_half, cross_half, weights = pl.pallas_call(
        functools.partial(up_kernel, members, slots),
        out_shape=[
            shape((members, vecs + vecs // 2, LANES), F32),
            shape((vecs, points // 2), F32),
            shape((vecs, points // 2), F32),
            held(4, groups, LANES, LANES),
        ],
        in_specs=[HBM_SPEC] * 5,
        out_specs=[VMEM_SPEC] * 4,
        scratch_shapes=[
            pltpu.VMEM((vecs, points), F32),
            pltpu.VMEM(basis.shape, F32),
            pltpu.VMEM(trans_blocks.shape, F32),
            pltpu.SMEM((slots, members), jnp.int32),
            pltpu.SMEM((1, members), jnp.int32),
            pltpu.VMEM((4 * node_groups + 8, vecs, LANES), F32),
            pltpu.SemaphoreType.DMA((7,)),
        ],
        compiler_params=params(8 + members // 4),
        name="up",
    )(
        in_hbm(vectors),
        in_hbm(basis),
        in_hbm(trans_blocks),
        in_hbm(jnp.transpose(send_node[0])),
        in_hbm(send_count),
    )
    incoming = lax.all_to_all(outgoing, BRANCH, split_axis=0, concat_axis=0, tiled=True)
    sub_got = lax.ppermute(sub_half, BRANCH, [(i, i ^ 1) for i in range(members)])
    pairs = [(i, i + 1) for i in range(1, members - 1, 2)]
    cross_got = lax.ppermute(cross_half, BRANCH, pairs + [(b, a) for a, b in pairs])

    near_scratch = [
        pltpu.VMEM((vecs, points), F32),
        pltpu.SMEM(near_src.shape[::-1], jnp.int32),
        pltpu.SMEM((1, leaf_dev), jnp.int32),
        pltpu.VMEM((leaf_dev // 2,) + near_mat.shape[1:], F32),
        pltpu.VMEM((2 * leaf_dev + 1, 2 * vecs, LANES), BF16),
        pltpu.SemaphoreType.DMA((3,)),
        pltpu.SemaphoreType.DMA((near_chunks,)),
    ]
    near_inputs = (
        in_hbm(vectors),
        in_hbm(jnp.transpose(near_src)),
        in_hbm(near_count.reshape(1, -1)),
        in_hbm(near_mat),
    )
    near, far_high, far_low = pl.pallas_call(
        functools.partial(first_kernel, members, slots),
        out_shape=[
            shape((vecs, points), F32),
            held(members + members // 4, LANES, LANES),
            held(members + members // 4, LANES, LANES),
        ],
        in_specs=[VMEM_SPEC] + [HBM_SPEC] * 7,
        out_specs=[VMEM_SPEC] * 3,
        scratch_shapes=[
            pltpu.VMEM(coup_blocks.shape, F32),
            pltpu.VMEM(upper_blocks.shape, F32),
            pltpu.VMEM(upper_coup.shape, F32),
            pltpu.SemaphoreType.DMA((3,)),
        ]
        + near_scratch,
        compiler_params=params(12 + members // 4),
        cost_estimate=cost(1 << 28, 16 << 20),
        name="near_first",
    )(sub_got, *near_inputs, in_hbm(coup_blocks), in_hbm(upper_blocks), in_hbm(upper_coup))
    near = pl.pallas_call(
        second_kernel,
        out_shape=shape((vecs, points), F32),
        in_specs=[VMEM_SPEC] + [HBM_SPEC] * 4 + [VMEM_SPEC],
        out_specs=VMEM_SPEC,
        scratch_shapes=near_scratch,
        input_output_aliases={5: 0},
        compiler_params=params(12),
        cost_estimate=cost(1 << 28, 8 << 20),
        name="near_second",
    )(cross_got, *near_inputs, near)

    return pl.pallas_call(
        functools.partial(down_kernel, members, slots),
        out_shape=shape((vecs, points), F32),
        in_specs=[VMEM_SPEC] * 5 + [HBM_SPEC],
        out_specs=VMEM_SPEC,
        scratch_shapes=[
            pltpu.SMEM((slots, members), jnp.int32),
            pltpu.VMEM((node_groups, vecs, LANES), F32),
            pltpu.VMEM((members, vecs, LANES), F32),
            pltpu.SemaphoreType.DMA((1,)),
        ],
        compiler_params=params(8 + members // 4),
        name="down",
    )(
        incoming,
        far_high,
        far_low,
        weights,
        near,
        in_hbm(jnp.transpose(coup_tgt[0])),
    )


def solution(mesh):
    spread = ("parts",) + BRANCH
    return jax.shard_map(
        body,
        mesh=mesh,
        in_specs=(
            P(None, spread),
            P(spread, None, None),
            P(spread, None, None, None, None),
            P("parts", None, None, None),
            P("parts", None, None),
            P(spread, None, None),
            P(spread, None),
            P(spread, None, None),
            P(spread, None, None, None, None),
            P(spread, None),
            P(spread),
            P(spread, None, None, None),
        ),
        out_specs=P(None, spread),
        check_vma=False,
    )
```

```python
import functools

import jax
import jax.numpy as jnp
from jax import lax
from jax.experimental import pallas as pl
from jax.experimental.pallas import tpu as pltpu
from jax.sharding import PartitionSpec as P

BRANCH = ("leaf", "sub")
LANES = 128
F32 = jnp.float32
BF16 = jnp.bfloat16
MIB = 1 << 20
AHEAD = 4


def split(x):
    high = x.astype(BF16)
    low = (x - high.astype(F32)).astype(BF16)
    return high, low


def contract_nt(a, b):
    return lax.dot_general(a, b, (((1,), (1,)), ((), ())), preferred_element_type=F32)


def contract_nn(a, b):
    return lax.dot_general(a, b, (((1,), (0,)), ((), ())), preferred_element_type=F32)


def contract_tn(a, b):
    return lax.dot_general(a, b, (((0,), (0,)), ((), ())), preferred_element_type=F32)


def times(x, high, low, dot):
    rows = x.shape[0]
    x_high, x_low = split(x)
    both = dot(jnp.concatenate([x_high, x_low], axis=0), high)
    return both[:rows] + both[rows:] + dot(x_high, low)


def product(a, b, dot):
    a_high, a_low = split(a)
    b_high, b_low = split(b)
    return dot(a_high, b_high) + (dot(a_high, b_low) + dot(a_low, b_high))


def lane_part(rows, part):
    return lax.broadcasted_iota(jnp.int32, (rows, LANES), 1) // part


def over(count, body, step=16):
    if count <= step:
        for i in range(count):
            body(i)
    else:

        def several(k, carry):
            for u in range(step):
                body(k * step + u)
            return carry

        lax.fori_loop(0, count // step, several, 0)


def fetch(sources, targets, semaphores):
    copies = []
    for i, (source, target) in enumerate(zip(sources, targets)):
        copies.append(pltpu.make_async_copy(source, target, semaphores.at[i]))
        copies[i].start()
    return copies


def up_kernel(
    members,
    slots,
    vec_far,
    basis_far,
    trans_far,
    send_node_far,
    send_count_far,
    upper_trans_far,
    upper_coup_far,
    outgoing,
    sub_half,
    cross_half,
    weights,
    upper_high,
    upper_low,
    upper_trans,
    couplers,
    vec,
    basis,
    trans,
    send_node,
    send_count,
    rolled,
    semaphores,
    upper_semaphores,
):
    position = lax.axis_index(BRANCH)
    half = vec.shape[1] // 2
    start = (position & 1) * half
    at_partner = vec_far.at[:, pl.ds(pl.multiple_of(half - start, LANES), half)]
    at_neighbour = vec_far.at[:, pl.ds(pl.multiple_of(start, LANES), half)]
    arriving = fetch(
        (vec_far, basis_far, trans_far, send_node_far, send_count_far, at_partner, at_neighbour),
        (vec, basis, trans, send_node, send_count, sub_half, cross_half),
        semaphores,
    )
    sources = [upper_trans_far]
    targets = [upper_trans]
    for j in range(couplers.shape[0]):
        sources.append(upper_coup_far.at[2 * members - 2 * (members >> j) + (position >> j)])
        targets.append(couplers.at[j])
    upper_arriving = fetch(sources, targets, upper_semaphores)
    basis_high, basis_low, trans_high, trans_low = (weights.at[i] for i in range(4))
    leaf_dev, rank, leaf_size = basis.shape
    vecs = vec.shape[0]
    left = lane_part(vecs, LANES // 2) == 0
    blank = jnp.zeros((rank, LANES // 2), F32)

    arriving[0].wait()
    arriving[1].wait()
    for leaf in range(leaf_dev):
        group, q = leaf // 4, leaf % 4
        high, low = split(jnp.concatenate([basis[leaf], blank] if q % 2 == 0 else [blank, basis[leaf]], axis=1))
        basis_high[group, q * rank : (q + 1) * rank] = high
        basis_low[group, q * rank : (q + 1) * rank] = low
    def keep(group, value):
        for k in range(4):
            rolled[4 * group + k] = value if k == 0 else pltpu.roll(value, k * rank, 1)

    def joined(first, second, high, low):
        both = times(jnp.concatenate([first, second], axis=0), high, low, contract_nt)
        return jnp.where(left, both[:vecs], both[vecs:])

    level = []
    for g in range(leaf_dev // 4):
        first = vec[:, 2 * LANES * g : 2 * LANES * g + LANES]
        second = vec[:, 2 * LANES * g + LANES : 2 * LANES * (g + 1)]
        level.append(joined(first, second, basis_high[g], basis_low[g]))
        keep(g, level[g])
    arriving[2].wait()
    for copy in upper_arriving:
        copy.wait()
    tops = map_tops(members, upper_trans, couplers, upper_high, upper_low)
    for node in range(leaf_dev):
        group, q = node // 4, node % 4
        if node < leaf_dev - 1:
            pair = [trans[2 * node], trans[2 * node + 1]]
            high, low = split(jnp.concatenate(pair + [blank] if q % 2 == 0 else [blank] + pair, axis=1))
        else:
            high = low = jnp.zeros((rank, LANES), BF16)
        trans_high[group, q * rank : (q + 1) * rank] = high
        trans_low[group, q * rank : (q + 1) * rank] = low
    done = leaf_dev // 4
    weight = 0
    while len(level) > 1:
        nodes = []
        for g in range(len(level) // 2):
            nodes.append(joined(level[2 * g], level[2 * g + 1], trans_high[weight], trans_low[weight]))
            keep(done, nodes[g])
            weight += 1
            done += 1
        level = nodes
        next(tops, None)
    two = jnp.where(left, times(level[0], trans_high[weight], trans_low[weight], contract_nt), 0.0)
    next(tops, None)
    top = times(two, trans_high[weight], trans_low[weight], contract_nt)
    for _ in tops:
        pass
    keep(done, jnp.where(left, two, top))
    blank_index = 4 * (done + 1)
    rolled[blank_index] = jnp.zeros((vecs, LANES), F32)

    arriving[3].wait()
    arriving[4].wait()
    part = lane_part(vecs, rank)
    few = lane_part(vecs // 2, rank)
    first = position & 3
    second = (position + 1) & 3
    top_rows = jnp.where(
        few == first,
        rolled[4 * done + ((first - 2) & 3), : vecs // 2],
        jnp.where(few == second, rolled[4 * done + ((second - 2) & 3), vecs // 2 :], 0.0),
    )

    def pick(target):
        count = send_count[0, target]
        value = None
        for j in range(slots):
            node = send_node[j, target]
            index = (node >> 2) * 4 + ((j - node) & 3)
            piece = rolled[jnp.where(j < count, index, blank_index)]
            value = piece if value is None else jnp.where(part == j, piece, value)
        outgoing[target, :vecs] = value
        outgoing[target, vecs:] = top_rows

    over(members, pick)
    arriving[5].wait()
    arriving[6].wait()


def pack_couplings(members, slots, coup_mat, coup):
    def one(source):
        blocks = [coup_mat[source * slots + j] for j in range(slots)]
        coup[0, source], coup[1, source] = split(jnp.concatenate(blocks, axis=1))

    over(members, one)


def map_tops(members, upper_trans, couplers, upper_high, upper_low):
    position = lax.axis_index(BRANCH)
    rank = upper_trans.shape[1]
    height = members.bit_length() - 1
    upper_high[...] = jnp.zeros(upper_high.shape, BF16)
    upper_low[...] = jnp.zeros(upper_low.shape, BF16)
    blank = jnp.zeros((rank, LANES - rank), F32)

    def place(group, value):
        high, low = split(value)
        upper_high[group, 2 * rank : 3 * rank] = high
        upper_low[group, 2 * rank : 3 * rank] = low

    def transfer(index, c):
        return upper_trans[index * 2 + c]

    def child(j):
        mixer = members - (members >> (j - 1)) + (position >> j)
        return transfer(mixer, (position >> (j - 1)) & 1)

    paths = [None, child(1)]
    current = [[(position ^ 1, couplers[0])]] + [None] * (height - 1)
    left_to_do = list(range(height))
    while any(left_to_do[1:]) or any(entry is None for entry in current):
        for j in range(1, height):
            if current[j] is not None and left_to_do[j] > 0:
                lower = left_to_do[j]
                offset = members - (members >> (lower - 1))
                following = []
                for index, matrix in current[j]:
                    for c in range(2):
                        mixed = product(matrix, transfer(offset + index, c), contract_nn)
                        following.append((2 * index + c, mixed))
                current[j] = following
                left_to_do[j] = lower - 1
        for j in range(1, min(len(paths), height)):
            if current[j] is None:
                current[j] = [((position >> j) ^ 1, product(paths[j], couplers[j], contract_tn))]
        if len(paths) < height:
            paths.append(product(child(len(paths)), paths[-1], contract_nn))
        yield
    own = jnp.zeros((rank, LANES), F32)
    for j in range(height):
        if j < 2:
            for index, matrix in current[j]:
                wide = jnp.concatenate([matrix, blank], axis=1)
                own = own + pltpu.roll(wide, (index & 3) * rank, 1)
        else:
            for k in range(0, len(current[j]), 4):
                wide = jnp.concatenate([matrix for _, matrix in current[j][k : k + 4]], axis=1)
                place(current[j][k][0] >> 2, wide)
    place(position >> 2, own)


def near_half(
    first,
    halo_half,
    vec_far,
    near_src_far,
    near_count_far,
    near_mat_far,
    near,
    vec,
    near_src,
    near_count,
    near_mat,
    values,
    semaphores,
    block_semaphores,
    ahead,
    before,
):
    position = lax.axis_index(BRANCH)
    leaves, near_slots, leaf_size, _ = near_mat.shape
    leaf_dev = near_src.shape[1]
    vecs = vec.shape[0]
    halo = leaf_dev // 2
    upper = (position & 1) ^ (1 if first else 0)
    base = upper * halo
    skip = 0 if first else ahead.shape[0]
    arriving = fetch((vec_far, near_src_far, near_count_far), (vec, near_src, near_count), semaphores)
    chunks = block_semaphores.shape[0]
    chunk = leaves // chunks

    def chunk_copy(k):
        here = pl.ds(k * chunk, chunk)
        return pltpu.make_async_copy(
            near_mat_far.at[pl.ds(base + skip + k * chunk, chunk)], near_mat.at[here], block_semaphores.at[k]
        )

    for k in range(chunks):
        chunk_copy(k).start()
    if first:
        others = near_mat_far.at[pl.ds(halo - base, ahead.shape[0])]
        ahead_copy = pltpu.make_async_copy(others, ahead, semaphores.at[len(arriving)])
        ahead_copy.start()
    before()
    for copy in arriving:
        copy.wait()
    left = lane_part(vecs, leaf_size) == 0

    def lay(base, block):
        for m in range(block.shape[1] // LANES):
            pair = block[:, m * LANES : (m + 1) * LANES]
            swapped = pltpu.roll(pair, leaf_size, 1)
            for c, twice in enumerate((jnp.where(left, pair, swapped), jnp.where(left, swapped, pair))):
                high, low = split(twice)
                values[base + 2 * m + c, :vecs] = high
                values[base + 2 * m + c, vecs:] = low

    lay(upper * (halo + leaf_dev), halo_half[...])
    lay(halo, vec[...])
    values[2 * leaf_dev] = jnp.zeros((2 * vecs, LANES), BF16)
    shift = halo - position * leaf_dev
    wide_left = lane_part(2 * vecs, leaf_size) == 0

    def source(leaf, slot):
        live = slot < near_count[0, base + leaf]
        return values[jnp.where(live, near_src[slot, base + leaf] + shift, 2 * leaf_dev)]

    def two_leaves(pair, blocks, start):
        total = None
        leaves = (2 * pair, 2 * pair + 1)
        for tile in range(0, near_slots, 4):
            columns = min(4, near_slots - tile)
            rows_x = []
            rows_w = []
            for leaf in leaves:
                xs = []
                ws = []
                for i in range(tile, tile + columns, 2):
                    if i + 1 < tile + columns:
                        xs.append(jnp.where(wide_left, source(leaf, i), source(leaf, i + 1)))
                        two = [blocks[leaf - start, i], blocks[leaf - start, i + 1]]
                        ws.append(jnp.concatenate(two, axis=1))
                    else:
                        xs.append(source(leaf, i))
                        blank = jnp.zeros((leaf_size, LANES - leaf_size), F32)
                        ws.append(jnp.concatenate([blocks[leaf - start, i], blank], axis=1))
                rows_x.append(jnp.concatenate(xs, axis=1) if len(xs) > 1 else xs[0])
                rows_w.append(jnp.concatenate(ws, axis=1) if len(ws) > 1 else ws[0])
            x = jnp.concatenate(rows_x, axis=0)
            high, low = split(jnp.concatenate(rows_w, axis=0))
            term = contract_nt(x, high) + contract_nt(x, low)
            total = term if total is None else total + term
        first = total[:vecs] + total[vecs : 2 * vecs]
        second = total[2 * vecs : 3 * vecs] + total[3 * vecs :]
        lanes = pl.ds(pl.multiple_of((base // 2 + pair) * LANES, LANES), LANES)
        near[:, lanes] = jnp.where(left, first, second)

    for pair in range(skip // 2):
        two_leaves(pair, ahead, 0)
    for k in range(chunks):
        chunk_copy(k).wait()
        for m in range(chunk // 2):
            two_leaves(skip // 2 + k * (chunk // 2) + m, near_mat, skip)
    if first:
        ahead_copy.wait()


def first_kernel(
    members,
    slots,
    halo_half,
    vec_far,
    near_src_far,
    near_count_far,
    near_mat_far,
    coup_mat_far,
    coup_tgt_far,
    near,
    coup,
    targets,
    ahead,
    coup_mat,
    coup_semaphores,
    *scratch,
):
    arriving = fetch((coup_mat_far, coup_tgt_far), (coup_mat, targets), coup_semaphores)

    def before():
        for copy in arriving:
            copy.wait()
        pack_couplings(members, slots, coup_mat, coup)

    near_half(True, halo_half, vec_far, near_src_far, near_count_far, near_mat_far, near, *scratch, ahead, before)


def second_kernel(
    halo_half, vec_far, near_src_far, near_count_far, near_mat_far, near_first, ahead, near, *scratch
):
    del near_first
    inputs = (halo_half, vec_far, near_src_far, near_count_far, near_mat_far)
    near_half(False, *inputs, near, *scratch, ahead, lambda: None)


def down_kernel(
    members,
    slots,
    incoming,
    coup,
    upper_high,
    upper_low,
    weights,
    near,
    targets,
    out,
    coup_tgt,
    parts_far,
    pieces,
    semaphores,
):
    arriving = fetch((targets,), (coup_tgt,), semaphores)
    basis_high, basis_low, trans_high, trans_low = (weights.at[i] for i in range(4))
    vecs = out.shape[0]
    rank = LANES // slots
    groups = parts_far.shape[1]
    parts_far[...] = jnp.zeros(parts_far.shape, F32)
    part = lane_part(vecs, rank)

    pieces[...] = jnp.zeros(pieces.shape, F32)

    def couple(source):
        values = incoming[source, :vecs]
        rows = jnp.concatenate([jnp.where(part == j, values, 0.0) for j in range(slots)], axis=0)
        pieces[source, :, :rank] = times(rows, coup[0, source], coup[1, source], contract_nt)

    over(members, couple)

    few = lane_part(vecs // 2, rank)
    term = jnp.zeros((vecs, LANES), F32)
    for g in range(members // 4):
        first = jnp.zeros((vecs // 2, LANES), F32)
        second = jnp.zeros((vecs // 2, LANES), F32)
        for q in range(4):
            rows = incoming[4 * g + q, vecs:]
            first = jnp.where(few == q, rows, first)
            second = jnp.where(few == (q + 1) % 4, rows, second)
        tops = jnp.concatenate([first, pltpu.roll(second, LANES - rank, 1)], axis=0)
        term = term + times(tops, upper_high[g], upper_low[g], contract_nt)
    arriving[0].wait()

    def scatter(source):
        for j in range(slots):
            node = coup_tgt[j, source]
            alone = pieces[source, j * vecs : (j + 1) * vecs]
            parts_far[j, node >> 2] += pltpu.roll(alone, (node & 3) * rank, 1)

    over(members, scatter)
    far = [sum(parts_far[j, g] for j in range(1, slots)) + parts_far[0, g] for g in range(groups)]

    left = part < 2
    weight = trans_high.shape[0] - 1

    def first_half(x):
        return jnp.where(left, x, 0.0)

    def second_half(x):
        return jnp.where(left, 0.0, x)

    def spread(x, high, low):
        both = times(jnp.concatenate([first_half(x), second_half(x)], axis=0), high, low, contract_nn)
        return both[:vecs], both[vecs:]

    first = groups - 2
    high, low = trans_high[weight], trans_low[weight]
    base = far[first + 1] + term
    two = base + times(second_half(base), high, low, contract_nn)
    level = [far[first] + times(first_half(two), high, low, contract_nn)]
    while first > 0:
        first -= 2 * len(level)
        weight -= len(level)
        children = []
        for g, value in enumerate(level):
            pair = spread(value, trans_high[weight + g], trans_low[weight + g])
            children.append(far[first + 2 * g] + pair[0])
            children.append(far[first + 2 * g + 1] + pair[1])
        level = children
    for g, value in enumerate(level):
        for c, points in enumerate(spread(value, basis_high[g], basis_low[g])):
            lanes = slice(LANES * (2 * g + c), LANES * (2 * g + c + 1))
            out[:, lanes] = near[:, lanes] + points


def in_hbm(x):
    return pltpu.with_memory_space_constraint(x, pltpu.HBM)


HBM_SPEC = pl.BlockSpec(memory_space=pltpu.HBM)
VMEM_SPEC = pl.BlockSpec(memory_space=pltpu.VMEM)


def params(mib):
    return pltpu.CompilerParams(vmem_limit_bytes=mib * MIB)


def cost(flops, size):
    return pl.CostEstimate(flops=flops, bytes_accessed=size, transcendentals=0)


def body(
    vectors,
    basis,
    trans,
    upper_trans,
    upper_coup,
    send_node,
    send_count,
    coup_tgt,
    coup_mat,
    near_src,
    near_count,
    near_mat,
):
    vecs, points = vectors.shape
    leaf_dev, rank, leaf_size = basis.shape
    members = lax.axis_size(BRANCH)
    slots = send_node.shape[2]
    groups = leaf_dev // 4
    node_groups = 2 * groups
    trans_blocks = trans.reshape(-1, rank, rank)
    coup_blocks = coup_mat.reshape(-1, rank, rank)
    upper_blocks = upper_trans.reshape(-1, rank, rank)
    near_chunks = leaf_dev // 16
    shape = jax.ShapeDtypeStruct

    def held(*dims):
        return shape(dims, BF16)

    height = members.bit_length() - 1
    outgoing, sub_half, cross_half, weights, upper_high, upper_low = pl.pallas_call(
        functools.partial(up_kernel, members, slots),
        out_shape=[
            shape((members, vecs + vecs // 2, LANES), F32),
            shape((vecs, points // 2), F32),
            shape((vecs, points // 2), F32),
            held(4, groups, LANES, LANES),
            held(members // 4, LANES, LANES),
            held(members // 4, LANES, LANES),
        ],
        in_specs=[HBM_SPEC] * 7,
        out_specs=[VMEM_SPEC] * 6,
        scratch_shapes=[
            pltpu.VMEM(upper_blocks.shape, F32),
            pltpu.VMEM((height, rank, rank), F32),
            pltpu.VMEM((vecs, points), F32),
            pltpu.VMEM(basis.shape, F32),
            pltpu.VMEM(trans_blocks.shape, F32),
            pltpu.SMEM((slots, members), jnp.int32),
            pltpu.SMEM((1, members), jnp.int32),
            pltpu.VMEM((4 * node_groups + 8, vecs, LANES), F32),
            pltpu.SemaphoreType.DMA((7,)),
            pltpu.SemaphoreType.DMA((1 + height,)),
        ],
        compiler_params=params(8 + members // 4),
        name="up",
    )(
        in_hbm(vectors),
        in_hbm(basis),
        in_hbm(trans_blocks),
        in_hbm(jnp.transpose(send_node[0])),
        in_hbm(send_count),
        in_hbm(upper_blocks),
        in_hbm(upper_coup),
    )
    incoming = lax.all_to_all(outgoing, BRANCH, split_axis=0, concat_axis=0, tiled=True)
    sub_got = lax.ppermute(sub_half, BRANCH, [(i, i ^ 1) for i in range(members)])
    pairs = [(i, i + 1) for i in range(1, members - 1, 2)]
    cross_got = lax.ppermute(cross_half, BRANCH, pairs + [(b, a) for a, b in pairs])

    def near_scratch(leaves):
        return [
            pltpu.VMEM((vecs, points), F32),
            pltpu.SMEM(near_src.shape[::-1], jnp.int32),
            pltpu.SMEM((1, leaf_dev), jnp.int32),
            pltpu.VMEM((leaves,) + near_mat.shape[1:], F32),
            pltpu.VMEM((2 * leaf_dev + 1, 2 * vecs, LANES), BF16),
            pltpu.SemaphoreType.DMA((4,)),
            pltpu.SemaphoreType.DMA((near_chunks,)),
        ]

    ahead_leaves = AHEAD
    near_inputs = (
        in_hbm(vectors),
        in_hbm(jnp.transpose(near_src)),
        in_hbm(near_count.reshape(1, -1)),
        in_hbm(near_mat),
    )
    near, coup, targets, ahead = pl.pallas_call(
        functools.partial(first_kernel, members, slots),
        out_shape=[
            shape((vecs, points), F32),
            held(2, members, rank, LANES),
            shape((slots, members), jnp.int32),
            shape((ahead_leaves,) + near_mat.shape[1:], F32),
        ],
        in_specs=[VMEM_SPEC] + [HBM_SPEC] * 6,
        out_specs=[VMEM_SPEC] * 4,
        scratch_shapes=[
            pltpu.VMEM(coup_blocks.shape, F32),
            pltpu.SemaphoreType.DMA((2,)),
        ]
        + near_scratch(leaf_dev // 2),
        compiler_params=params(12 + members // 4),
        cost_estimate=cost(1 << 28, 16 << 20),
        name="near_first",
    )(
        sub_got,
        *near_inputs,
        in_hbm(coup_blocks),
        in_hbm(jnp.transpose(coup_tgt[0])),
    )

    near = pl.pallas_call(
        second_kernel,
        out_shape=shape((vecs, points), F32),
        in_specs=[VMEM_SPEC] + [HBM_SPEC] * 4 + [VMEM_SPEC] * 2,
        out_specs=VMEM_SPEC,
        scratch_shapes=near_scratch(leaf_dev // 2 - ahead_leaves),
        input_output_aliases={5: 0},
        compiler_params=params(12 + members // 4),
        cost_estimate=cost(1 << 28, 8 << 20),
        name="near_second",
    )(cross_got, *near_inputs, near, ahead)

    return pl.pallas_call(
        functools.partial(down_kernel, members, slots),
        out_shape=shape((vecs, points), F32),
        in_specs=[VMEM_SPEC] * 7,
        out_specs=VMEM_SPEC,
        scratch_shapes=[
            pltpu.SMEM((slots, members), jnp.int32),
            pltpu.VMEM((slots, node_groups, vecs, LANES), F32),
            pltpu.VMEM((members, slots * vecs, LANES), F32),
            pltpu.SemaphoreType.DMA((1,)),
        ],
        compiler_params=params(8 + members // 4),
        name="down",
    )(
        incoming,
        coup,
        upper_high,
        upper_low,
        weights,
        near,
        targets,
    )


def solution(mesh):
    spread = ("parts",) + BRANCH
    return jax.shard_map(
        body,
        mesh=mesh,
        in_specs=(
            P(None, spread),
            P(spread, None, None),
            P(spread, None, None, None, None),
            P("parts", None, None, None),
            P("parts", None, None),
            P(spread, None, None),
            P(spread, None),
            P(spread, None, None),
            P(spread, None, None, None, None),
            P(spread, None),
            P(spread),
            P(spread, None, None, None),
        ),
        out_specs=P(None, spread),
        check_vma=False,
    )
```

```python
import functools

import jax
import jax.numpy as jnp
from jax import lax
from jax.experimental import pallas as pl
from jax.experimental.pallas import tpu as pltpu
from jax.sharding import PartitionSpec as P

BRANCH = ("leaf", "sub")
LANES = 128
F32 = jnp.float32
BF16 = jnp.bfloat16
MIB = 1 << 20
AHEAD = 6


def split(x):
    high = x.astype(BF16)
    low = (x - high.astype(F32)).astype(BF16)
    return high, low


def contract_nt(a, b):
    return lax.dot_general(a, b, (((1,), (1,)), ((), ())), preferred_element_type=F32)


def contract_nn(a, b):
    return lax.dot_general(a, b, (((1,), (0,)), ((), ())), preferred_element_type=F32)


def contract_tn(a, b):
    return lax.dot_general(a, b, (((0,), (0,)), ((), ())), preferred_element_type=F32)


def times(x, high, low, dot):
    rows = x.shape[0]
    x_high, x_low = split(x)
    both = dot(jnp.concatenate([x_high, x_low], axis=0), high)
    return both[:rows] + both[rows:] + dot(x_high, low)


def product(a, b, dot):
    a_high, a_low = split(a)
    b_high, b_low = split(b)
    return dot(a_high, b_high) + (dot(a_high, b_low) + dot(a_low, b_high))


def lane_part(rows, part):
    return lax.broadcasted_iota(jnp.int32, (rows, LANES), 1) // part


def over(count, body, step=16):
    if count <= step:
        for i in range(count):
            body(i)
    else:

        def several(k, carry):
            for u in range(step):
                body(k * step + u)
            return carry

        lax.fori_loop(0, count // step, several, 0)


def fetch(sources, targets, semaphores):
    copies = []
    for i, (source, target) in enumerate(zip(sources, targets)):
        copies.append(pltpu.make_async_copy(source, target, semaphores.at[i]))
        copies[i].start()
    return copies


def up_kernel(
    members,
    slots,
    vec_far,
    basis_far,
    trans_far,
    send_node_far,
    send_count_far,
    upper_trans_far,
    upper_coup_far,
    outgoing,
    sub_half,
    cross_half,
    weights,
    upper,
    upper_trans,
    couplers,
    vec,
    basis,
    trans,
    send_node,
    send_count,
    rolled,
    semaphores,
    upper_semaphores,
):
    position = lax.axis_index(BRANCH)
    half = vec.shape[1] // 2
    start = (position & 1) * half
    at_partner = vec_far.at[:, pl.ds(pl.multiple_of(half - start, LANES), half)]
    at_neighbour = vec_far.at[:, pl.ds(pl.multiple_of(start, LANES), half)]
    arriving = fetch(
        (vec_far, basis_far, trans_far, send_node_far, send_count_far, at_partner, at_neighbour),
        (vec, basis, trans, send_node, send_count, sub_half, cross_half),
        semaphores,
    )
    sources = [upper_trans_far]
    targets = [upper_trans]
    for j in range(couplers.shape[0]):
        sources.append(upper_coup_far.at[2 * members - 2 * (members >> j) + (position >> j)])
        targets.append(couplers.at[j])
    upper_arriving = fetch(sources, targets, upper_semaphores)
    basis_high, basis_low, trans_high, trans_low = (weights.at[i] for i in range(4))
    leaf_dev, rank, leaf_size = basis.shape
    vecs = vec.shape[0]
    left = lane_part(vecs, LANES // 2) == 0
    blank = jnp.zeros((rank, LANES // 2), F32)

    arriving[0].wait()
    arriving[1].wait()
    for leaf in range(leaf_dev):
        group, q = leaf // 4, leaf % 4
        high, low = split(jnp.concatenate([basis[leaf], blank] if q % 2 == 0 else [blank, basis[leaf]], axis=1))
        basis_high[group, q * rank : (q + 1) * rank] = high
        basis_low[group, q * rank : (q + 1) * rank] = low
    def keep(group, value):
        for k in range(4):
            rolled[4 * group + k] = value if k == 0 else pltpu.roll(value, k * rank, 1)

    def joined(first, second, high, low):
        both = times(jnp.concatenate([first, second], axis=0), high, low, contract_nt)
        return jnp.where(left, both[:vecs], both[vecs:])

    level = []
    for g in range(leaf_dev // 4):
        first = vec[:, 2 * LANES * g : 2 * LANES * g + LANES]
        second = vec[:, 2 * LANES * g + LANES : 2 * LANES * (g + 1)]
        level.append(joined(first, second, basis_high[g], basis_low[g]))
        keep(g, level[g])
    arriving[2].wait()
    for copy in upper_arriving:
        copy.wait()
    arriving[3].wait()
    arriving[4].wait()
    tops = map_tops(members, upper_trans, couplers, upper)
    for node in range(leaf_dev):
        group, q = node // 4, node % 4
        if node < leaf_dev - 1:
            pair = [trans[2 * node], trans[2 * node + 1]]
            high, low = split(jnp.concatenate(pair + [blank] if q % 2 == 0 else [blank] + pair, axis=1))
        else:
            high = low = jnp.zeros((rank, LANES), BF16)
        trans_high[group, q * rank : (q + 1) * rank] = high
        trans_low[group, q * rank : (q + 1) * rank] = low
    done = leaf_dev // 4
    weight = 0
    while len(level) > 1:
        nodes = []
        for g in range(len(level) // 2):
            nodes.append(joined(level[2 * g], level[2 * g + 1], trans_high[weight], trans_low[weight]))
            keep(done, nodes[g])
            weight += 1
            done += 1
        level = nodes
        next(tops, None)
    two = jnp.where(left, times(level[0], trans_high[weight], trans_low[weight], contract_nt), 0.0)
    next(tops, None)
    top = times(two, trans_high[weight], trans_low[weight], contract_nt)
    for _ in tops:
        pass
    keep(done, jnp.where(left, two, top))
    blank_index = 4 * (done + 1)
    rolled[blank_index] = jnp.zeros((vecs, LANES), F32)

    part = lane_part(vecs, rank)
    few = lane_part(vecs // 2, rank)
    first = position & 3
    second = (position + 1) & 3
    top_rows = jnp.where(
        few == first,
        rolled[4 * done + ((first - 2) & 3), : vecs // 2],
        jnp.where(few == second, rolled[4 * done + ((second - 2) & 3), vecs // 2 :], 0.0),
    )

    def pick(target):
        count = send_count[0, target]
        value = None
        for j in range(slots):
            node = send_node[j, target]
            index = (node >> 2) * 4 + ((j - node) & 3)
            piece = rolled[jnp.where(j < count, index, blank_index)]
            value = piece if value is None else jnp.where(part == j, piece, value)
        outgoing[target, :vecs] = value
        outgoing[target, vecs:] = top_rows

    over(members, pick)
    arriving[5].wait()
    arriving[6].wait()


def pack_couplings(members, slots, coup_mat, coup):
    def one(source):
        blocks = [coup_mat[source * slots + j] for j in range(slots)]
        coup[0, source], coup[1, source] = split(jnp.concatenate(blocks, axis=1))

    over(members, one)


def map_tops(members, upper_trans, couplers, upper):
    position = lax.axis_index(BRANCH)
    rank = upper_trans.shape[1]
    height = members.bit_length() - 1
    blank = jnp.zeros((rank, LANES - rank), F32)

    def place(group, value):
        upper[0, group], upper[1, group] = split(value)

    def transfer(index, c):
        return upper_trans[index * 2 + c]

    def child(j):
        mixer = members - (members >> (j - 1)) + (position >> j)
        return transfer(mixer, (position >> (j - 1)) & 1)

    paths = [None, child(1)]
    current = [[(position ^ 1, couplers[0])]] + [None] * (height - 1)
    left_to_do = list(range(height))
    while any(left_to_do[1:]) or any(entry is None for entry in current):
        for j in range(1, height):
            if current[j] is not None and left_to_do[j] > 0:
                lower = left_to_do[j]
                offset = members - (members >> (lower - 1))
                following = []
                for index, matrix in current[j]:
                    for c in range(2):
                        mixed = product(matrix, transfer(offset + index, c), contract_nn)
                        following.append((2 * index + c, mixed))
                current[j] = following
                left_to_do[j] = lower - 1
        for j in range(1, min(len(paths), height)):
            if current[j] is None:
                current[j] = [((position >> j) ^ 1, product(paths[j], couplers[j], contract_tn))]
        if len(paths) < height:
            paths.append(product(child(len(paths)), paths[-1], contract_nn))
        yield
    own = jnp.zeros((rank, LANES), F32)
    for j in range(height):
        if j < 2:
            for index, matrix in current[j]:
                wide = jnp.concatenate([matrix, blank], axis=1)
                own = own + pltpu.roll(wide, (index & 3) * rank, 1)
        else:
            for k in range(0, len(current[j]), 4):
                wide = jnp.concatenate([matrix for _, matrix in current[j][k : k + 4]], axis=1)
                place(current[j][k][0] >> 2, wide)
    place(position >> 2, own)


def near_half(
    first,
    halo_half,
    vec_far,
    near_src_far,
    near_count_far,
    near_mat_far,
    near,
    vec,
    near_src,
    near_count,
    near_mat,
    values,
    semaphores,
    block_semaphores,
    ahead,
    before,
):
    position = lax.axis_index(BRANCH)
    leaves, near_slots, leaf_size, _ = near_mat.shape
    leaf_dev = near_src.shape[1]
    vecs = vec.shape[0]
    halo = leaf_dev // 2
    upper = (position & 1) ^ (1 if first else 0)
    base = upper * halo
    skip = 0 if first else ahead.shape[0]
    arriving = fetch((vec_far, near_src_far, near_count_far), (vec, near_src, near_count), semaphores)
    sizes = ((leaves + 3) // 4 * 2, leaves - (leaves + 3) // 4 * 2)

    def chunk_copy(k):
        start = k * sizes[0]
        there = near_mat_far.at[pl.ds(base + skip + start, sizes[k])]
        return pltpu.make_async_copy(there, near_mat.at[pl.ds(start, sizes[k])], block_semaphores.at[k])

    for k in range(2):
        chunk_copy(k).start()
    if first:
        others = near_mat_far.at[pl.ds(halo - base, ahead.shape[0])]
        ahead_copy = pltpu.make_async_copy(others, ahead, semaphores.at[len(arriving)])
        ahead_copy.start()
    before()
    for copy in arriving:
        copy.wait()
    left = lane_part(vecs, leaf_size) == 0

    def lay(base, block):
        for m in range(block.shape[1] // LANES):
            pair = block[:, m * LANES : (m + 1) * LANES]
            swapped = pltpu.roll(pair, leaf_size, 1)
            for c, twice in enumerate((jnp.where(left, pair, swapped), jnp.where(left, swapped, pair))):
                high, low = split(twice)
                values[base + 2 * m + c, :vecs] = high
                values[base + 2 * m + c, vecs:] = low

    lay(upper * (halo + leaf_dev), halo_half[...])
    lay(halo, vec[...])
    values[2 * leaf_dev] = jnp.zeros((2 * vecs, LANES), BF16)
    shift = halo - position * leaf_dev
    wide_left = lane_part(2 * vecs, leaf_size) == 0

    def source(leaf, slot):
        live = slot < near_count[0, base + leaf]
        return values[jnp.where(live, near_src[slot, base + leaf] + shift, 2 * leaf_dev)]

    def two_leaves(pair, blocks, start):
        total = None
        leaves = (2 * pair, 2 * pair + 1)
        for tile in range(0, near_slots, 4):
            columns = min(4, near_slots - tile)
            rows_x = []
            rows_w = []
            for leaf in leaves:
                xs = []
                ws = []
                for i in range(tile, tile + columns, 2):
                    if i + 1 < tile + columns:
                        xs.append(jnp.where(wide_left, source(leaf, i), source(leaf, i + 1)))
                        two = [blocks[leaf - start, i], blocks[leaf - start, i + 1]]
                        ws.append(jnp.concatenate(two, axis=1))
                    else:
                        xs.append(source(leaf, i))
                        blank = jnp.zeros((leaf_size, LANES - leaf_size), F32)
                        ws.append(jnp.concatenate([blocks[leaf - start, i], blank], axis=1))
                rows_x.append(jnp.concatenate(xs, axis=1) if len(xs) > 1 else xs[0])
                rows_w.append(jnp.concatenate(ws, axis=1) if len(ws) > 1 else ws[0])
            x = jnp.concatenate(rows_x, axis=0)
            high, low = split(jnp.concatenate(rows_w, axis=0))
            term = contract_nt(x, high) + contract_nt(x, low)
            total = term if total is None else total + term
        first = total[:vecs] + total[vecs : 2 * vecs]
        second = total[2 * vecs : 3 * vecs] + total[3 * vecs :]
        lanes = pl.ds(pl.multiple_of((base // 2 + pair) * LANES, LANES), LANES)
        near[:, lanes] = jnp.where(left, first, second)

    for pair in range(skip // 2):
        two_leaves(pair, ahead, 0)
    for k in range(2):
        chunk_copy(k).wait()
        for m in range(sizes[k] // 2):
            two_leaves((skip + k * sizes[0]) // 2 + m, near_mat, skip)
    if first:
        ahead_copy.wait()


def first_kernel(
    members,
    slots,
    halo_half,
    vec_far,
    near_src_far,
    near_count_far,
    near_mat_far,
    coup_mat_far,
    coup_tgt_far,
    near,
    coup,
    targets,
    ahead,
    coup_mat,
    coup_semaphores,
    *scratch,
):
    arriving = fetch((coup_mat_far, coup_tgt_far), (coup_mat, targets), coup_semaphores)

    def before():
        for copy in arriving:
            copy.wait()
        pack_couplings(members, slots, coup_mat, coup)

    near_half(True, halo_half, vec_far, near_src_far, near_count_far, near_mat_far, near, *scratch, ahead, before)


def second_kernel(
    halo_half, vec_far, near_src_far, near_count_far, near_mat_far, near_first, ahead, near, *scratch
):
    del near_first
    inputs = (halo_half, vec_far, near_src_far, near_count_far, near_mat_far)
    near_half(False, *inputs, near, *scratch, ahead, lambda: None)


def down_kernel(
    members,
    slots,
    incoming,
    coup,
    upper,
    weights,
    near,
    targets,
    out,
    coup_tgt,
    parts_far,
    pieces,
    semaphores,
):
    arriving = fetch((targets,), (coup_tgt,), semaphores)
    basis_high, basis_low, trans_high, trans_low = (weights.at[i] for i in range(4))
    vecs = out.shape[0]
    rank = LANES // slots
    groups = parts_far.shape[1]
    parts_far[...] = jnp.zeros(parts_far.shape, F32)
    part = lane_part(vecs, rank)

    pieces[...] = jnp.zeros(pieces.shape, F32)

    def couple(source):
        values = incoming[source, :vecs]
        rows = jnp.concatenate([jnp.where(part == j, values, 0.0) for j in range(slots)], axis=0)
        pieces[source, :, :rank] = times(rows, coup[0, source], coup[1, source], contract_nt)

    over(members, couple)

    few = lane_part(vecs // 2, rank)
    term = jnp.zeros((vecs, rank), F32)
    for g in range(members // 4):
        first = jnp.zeros((vecs // 2, LANES), F32)
        second = jnp.zeros((vecs // 2, LANES), F32)
        for q in range(4):
            rows = incoming[4 * g + q, vecs:]
            first = jnp.where(few == q, rows, first)
            second = jnp.where(few == (q + 1) % 4, rows, second)
        tops = jnp.concatenate([first, pltpu.roll(second, LANES - rank, 1)], axis=0)
        term = term + times(tops, upper[0, g], upper[1, g], contract_nt)
    sides = [jnp.zeros((vecs, 2 * rank), F32), term, jnp.zeros((vecs, rank), F32)]
    term = jnp.concatenate(sides, axis=1)
    arriving[0].wait()

    def scatter(source):
        for j in range(slots):
            node = coup_tgt[j, source]
            alone = pieces[source, j * vecs : (j + 1) * vecs]
            parts_far[j, node >> 2] += pltpu.roll(alone, (node & 3) * rank, 1)

    over(members, scatter)
    far = [sum(parts_far[j, g] for j in range(1, slots)) + parts_far[0, g] for g in range(groups)]

    left = part < 2
    weight = trans_high.shape[0] - 1

    def first_half(x):
        return jnp.where(left, x, 0.0)

    def second_half(x):
        return jnp.where(left, 0.0, x)

    def spread(x, high, low):
        both = times(jnp.concatenate([first_half(x), second_half(x)], axis=0), high, low, contract_nn)
        return both[:vecs], both[vecs:]

    first = groups - 2
    high, low = trans_high[weight], trans_low[weight]
    base = far[first + 1] + term
    two = base + times(second_half(base), high, low, contract_nn)
    level = [far[first] + times(first_half(two), high, low, contract_nn)]
    while first > 0:
        first -= 2 * len(level)
        weight -= len(level)
        children = []
        for g, value in enumerate(level):
            pair = spread(value, trans_high[weight + g], trans_low[weight + g])
            children.append(far[first + 2 * g] + pair[0])
            children.append(far[first + 2 * g + 1] + pair[1])
        level = children
    for g, value in enumerate(level):
        for c, points in enumerate(spread(value, basis_high[g], basis_low[g])):
            lanes = slice(LANES * (2 * g + c), LANES * (2 * g + c + 1))
            out[:, lanes] = near[:, lanes] + points


def in_hbm(x):
    return pltpu.with_memory_space_constraint(x, pltpu.HBM)


HBM_SPEC = pl.BlockSpec(memory_space=pltpu.HBM)
VMEM_SPEC = pl.BlockSpec(memory_space=pltpu.VMEM)


def params(mib):
    return pltpu.CompilerParams(vmem_limit_bytes=mib * MIB)


def cost(flops, size):
    return pl.CostEstimate(flops=flops, bytes_accessed=size, transcendentals=0)


def body(
    vectors,
    basis,
    trans,
    upper_trans,
    upper_coup,
    send_node,
    send_count,
    coup_tgt,
    coup_mat,
    near_src,
    near_count,
    near_mat,
):
    vecs, points = vectors.shape
    leaf_dev, rank, leaf_size = basis.shape
    members = lax.axis_size(BRANCH)
    slots = send_node.shape[2]
    groups = leaf_dev // 4
    node_groups = 2 * groups
    trans_blocks = trans.reshape(-1, rank, rank)
    coup_blocks = coup_mat.reshape(-1, rank, rank)
    upper_blocks = upper_trans.reshape(-1, rank, rank)
    shape = jax.ShapeDtypeStruct

    def held(*dims):
        return shape(dims, BF16)

    height = members.bit_length() - 1
    outgoing, sub_half, cross_half, weights, upper = pl.pallas_call(
        functools.partial(up_kernel, members, slots),
        out_shape=[
            shape((members, vecs + vecs // 2, LANES), F32),
            shape((vecs, points // 2), F32),
            shape((vecs, points // 2), F32),
            held(4, groups, LANES, LANES),
            held(2, members // 4, rank, LANES),
        ],
        in_specs=[HBM_SPEC] * 7,
        out_specs=[VMEM_SPEC] * 5,
        scratch_shapes=[
            pltpu.VMEM(upper_blocks.shape, F32),
            pltpu.VMEM((height, rank, rank), F32),
            pltpu.VMEM((vecs, points), F32),
            pltpu.VMEM(basis.shape, F32),
            pltpu.VMEM(trans_blocks.shape, F32),
            pltpu.SMEM((slots, members), jnp.int32),
            pltpu.SMEM((1, members), jnp.int32),
            pltpu.VMEM((4 * node_groups + 8, vecs, LANES), F32),
            pltpu.SemaphoreType.DMA((7,)),
            pltpu.SemaphoreType.DMA((1 + height,)),
        ],
        compiler_params=params(8 + members // 4),
        name="up",
    )(
        in_hbm(vectors),
        in_hbm(basis),
        in_hbm(trans_blocks),
        in_hbm(jnp.transpose(send_node[0])),
        in_hbm(send_count),
        in_hbm(upper_blocks),
        in_hbm(upper_coup),
    )
    incoming = lax.all_to_all(outgoing, BRANCH, split_axis=0, concat_axis=0, tiled=True)
    sub_got = lax.ppermute(sub_half, BRANCH, [(i, i ^ 1) for i in range(members)])
    pairs = [(i, i + 1) for i in range(1, members - 1, 2)]
    cross_got = lax.ppermute(cross_half, BRANCH, pairs + [(b, a) for a, b in pairs])

    def near_scratch(leaves):
        return [
            pltpu.VMEM((vecs, points), F32),
            pltpu.SMEM(near_src.shape[::-1], jnp.int32),
            pltpu.SMEM((1, leaf_dev), jnp.int32),
            pltpu.VMEM((leaves,) + near_mat.shape[1:], F32),
            pltpu.VMEM((2 * leaf_dev + 1, 2 * vecs, LANES), BF16),
            pltpu.SemaphoreType.DMA((4,)),
            pltpu.SemaphoreType.DMA((2,)),
        ]

    ahead_leaves = AHEAD
    near_inputs = (
        in_hbm(vectors),
        in_hbm(jnp.transpose(near_src)),
        in_hbm(near_count.reshape(1, -1)),
        in_hbm(near_mat),
    )
    near, coup, targets, ahead = pl.pallas_call(
        functools.partial(first_kernel, members, slots),
        out_shape=[
            shape((vecs, points), F32),
            held(2, members, rank, LANES),
            shape((slots, members), jnp.int32),
            shape((ahead_leaves,) + near_mat.shape[1:], F32),
        ],
        in_specs=[VMEM_SPEC] + [HBM_SPEC] * 6,
        out_specs=[VMEM_SPEC] * 4,
        scratch_shapes=[
            pltpu.VMEM(coup_blocks.shape, F32),
            pltpu.SemaphoreType.DMA((2,)),
        ]
        + near_scratch(leaf_dev // 2),
        compiler_params=params(12 + members // 4),
        cost_estimate=cost(1 << 28, 16 << 20),
        name="near_first",
    )(
        sub_got,
        *near_inputs,
        in_hbm(coup_blocks),
        in_hbm(jnp.transpose(coup_tgt[0])),
    )

    near = pl.pallas_call(
        second_kernel,
        out_shape=shape((vecs, points), F32),
        in_specs=[VMEM_SPEC] + [HBM_SPEC] * 4 + [VMEM_SPEC] * 2,
        out_specs=VMEM_SPEC,
        scratch_shapes=near_scratch(leaf_dev // 2 - ahead_leaves),
        input_output_aliases={5: 0},
        compiler_params=params(12 + members // 4),
        cost_estimate=cost(1 << 28, 8 << 20),
        name="near_second",
    )(cross_got, *near_inputs, near, ahead)

    return pl.pallas_call(
        functools.partial(down_kernel, members, slots),
        out_shape=shape((vecs, points), F32),
        in_specs=[VMEM_SPEC] * 6,
        out_specs=VMEM_SPEC,
        scratch_shapes=[
            pltpu.SMEM((slots, members), jnp.int32),
            pltpu.VMEM((slots, node_groups, vecs, LANES), F32),
            pltpu.VMEM((members, slots * vecs, LANES), F32),
            pltpu.SemaphoreType.DMA((1,)),
        ],
        compiler_params=params(8 + members // 4),
        name="down",
    )(
        incoming,
        coup,
        upper,
        weights,
        near,
        targets,
    )


def solution(mesh):
    spread = ("parts",) + BRANCH
    return jax.shard_map(
        body,
        mesh=mesh,
        in_specs=(
            P(None, spread),
            P(spread, None, None),
            P(spread, None, None, None, None),
            P("parts", None, None, None),
            P("parts", None, None),
            P(spread, None, None),
            P(spread, None),
            P(spread, None, None),
            P(spread, None, None, None, None),
            P(spread, None),
            P(spread),
            P(spread, None, None, None),
        ),
        out_specs=P(None, spread),
        check_vma=False,
    )
```

```python
import functools

import jax
import jax.numpy as jnp
from jax import lax
from jax.experimental import pallas as pl
from jax.experimental.pallas import tpu as pltpu
from jax.sharding import PartitionSpec as P

BRANCH = ("leaf", "sub")
LANES = 128
F32 = jnp.float32
BF16 = jnp.bfloat16
MIB = 1 << 20
AHEAD = 6


def split(x):
    high = x.astype(BF16)
    low = (x - high.astype(F32)).astype(BF16)
    return high, low


def contract_nt(a, b):
    return lax.dot_general(a, b, (((1,), (1,)), ((), ())), preferred_element_type=F32)


def contract_nn(a, b):
    return lax.dot_general(a, b, (((1,), (0,)), ((), ())), preferred_element_type=F32)


def contract_tn(a, b):
    return lax.dot_general(a, b, (((0,), (0,)), ((), ())), preferred_element_type=F32)


def times(x, high, low, dot):
    rows = x.shape[0]
    x_high, x_low = split(x)
    both = dot(jnp.concatenate([x_high, x_low], axis=0), high)
    return both[:rows] + both[rows:] + dot(x_high, low)


def product(a, b, dot):
    a_high, a_low = split(a)
    b_high, b_low = split(b)
    return dot(a_high, b_high) + (dot(a_high, b_low) + dot(a_low, b_high))


def lane_part(rows, part):
    return lax.broadcasted_iota(jnp.int32, (rows, LANES), 1) // part


def over(count, body, step=16):
    if count <= step:
        for i in range(count):
            body(i)
    else:

        def several(k, carry):
            for u in range(step):
                body(k * step + u)
            return carry

        lax.fori_loop(0, count // step, several, 0)


def fetch(sources, targets, semaphores):
    copies = []
    for i, (source, target) in enumerate(zip(sources, targets)):
        copies.append(pltpu.make_async_copy(source, target, semaphores.at[i]))
        copies[i].start()
    return copies


def up_kernel(
    members,
    slots,
    vec_far,
    basis_far,
    trans_far,
    send_node_far,
    send_count_far,
    upper_trans_far,
    upper_coup_far,
    outgoing,
    sub_half,
    cross_half,
    weights,
    upper,
    upper_trans,
    couplers,
    vec,
    basis,
    trans,
    send_node,
    send_count,
    rolled,
    semaphores,
    upper_semaphores,
):
    position = lax.axis_index(BRANCH)
    half = vec.shape[1] // 2
    start = (position & 1) * half
    at_partner = vec_far.at[:, pl.ds(pl.multiple_of(half - start, LANES), half)]
    at_neighbour = vec_far.at[:, pl.ds(pl.multiple_of(start, LANES), half)]
    wanted = fetch((vec_far, basis_far), (vec, basis), semaphores)
    sources = [upper_trans_far]
    targets = [upper_trans]
    for j in range(couplers.shape[0]):
        sources.append(upper_coup_far.at[2 * members - 2 * (members >> j) + (position >> j)])
        targets.append(couplers.at[j])
    upper_arriving = fetch(sources, targets, upper_semaphores)
    others = fetch(
        (trans_far, send_node_far, send_count_far, at_partner, at_neighbour),
        (trans, send_node, send_count, sub_half, cross_half),
        semaphores.at[pl.ds(2, 5)],
    )
    arriving = wanted + others
    basis_high, basis_low, trans_high, trans_low = (weights.at[i] for i in range(4))
    leaf_dev, rank, leaf_size = basis.shape
    vecs = vec.shape[0]
    left = lane_part(vecs, LANES // 2) == 0
    blank = jnp.zeros((rank, LANES // 2), F32)

    arriving[0].wait()
    arriving[1].wait()
    for leaf in range(leaf_dev):
        group, q = leaf // 4, leaf % 4
        high, low = split(jnp.concatenate([basis[leaf], blank] if q % 2 == 0 else [blank, basis[leaf]], axis=1))
        basis_high[group, q * rank : (q + 1) * rank] = high
        basis_low[group, q * rank : (q + 1) * rank] = low
    def keep(group, value):
        for k in range(4):
            rolled[4 * group + k] = value if k == 0 else pltpu.roll(value, k * rank, 1)

    def joined(first, second, high, low):
        both = times(jnp.concatenate([first, second], axis=0), high, low, contract_nt)
        return jnp.where(left, both[:vecs], both[vecs:])

    level = []
    for g in range(leaf_dev // 4):
        first = vec[:, 2 * LANES * g : 2 * LANES * g + LANES]
        second = vec[:, 2 * LANES * g + LANES : 2 * LANES * (g + 1)]
        level.append(joined(first, second, basis_high[g], basis_low[g]))
        keep(g, level[g])
    arriving[2].wait()
    for copy in upper_arriving:
        copy.wait()
    arriving[3].wait()
    arriving[4].wait()
    tops = map_tops(members, upper_trans, couplers, upper)
    for node in range(leaf_dev):
        group, q = node // 4, node % 4
        if node < leaf_dev - 1:
            pair = [trans[2 * node], trans[2 * node + 1]]
            high, low = split(jnp.concatenate(pair + [blank] if q % 2 == 0 else [blank] + pair, axis=1))
        else:
            high = low = jnp.zeros((rank, LANES), BF16)
        trans_high[group, q * rank : (q + 1) * rank] = high
        trans_low[group, q * rank : (q + 1) * rank] = low
    done = leaf_dev // 4
    weight = 0
    while len(level) > 1:
        nodes = []
        next(tops, None)
        for g in range(len(level) // 2):
            nodes.append(joined(level[2 * g], level[2 * g + 1], trans_high[weight], trans_low[weight]))
            keep(done, nodes[g])
            weight += 1
            done += 1
        level = nodes
    two = jnp.where(left, times(level[0], trans_high[weight], trans_low[weight], contract_nt), 0.0)
    next(tops, None)
    top = times(two, trans_high[weight], trans_low[weight], contract_nt)
    for _ in tops:
        pass
    keep(done, jnp.where(left, two, top))
    blank_index = 4 * (done + 1)
    rolled[blank_index] = jnp.zeros((vecs, LANES), F32)

    part = lane_part(vecs, rank)
    few = lane_part(vecs // 2, rank)
    first = position & 3
    second = (position + 1) & 3
    top_rows = jnp.where(
        few == first,
        rolled[4 * done + ((first - 2) & 3), : vecs // 2],
        jnp.where(few == second, rolled[4 * done + ((second - 2) & 3), vecs // 2 :], 0.0),
    )

    def pick(target):
        count = send_count[0, target]
        value = None
        for j in range(slots):
            node = send_node[j, target]
            index = (node >> 2) * 4 + ((j - node) & 3)
            piece = rolled[jnp.where(j < count, index, blank_index)]
            value = piece if value is None else jnp.where(part == j, piece, value)
        outgoing[target, :vecs] = value
        outgoing[target, vecs:] = top_rows

    over(members, pick)
    arriving[5].wait()
    arriving[6].wait()


def pack_couplings(members, slots, coup_mat, coup):
    def one(source):
        blocks = [coup_mat[source * slots + j] for j in range(slots)]
        coup[0, source], coup[1, source] = split(jnp.concatenate(blocks, axis=1))

    over(members, one)


def map_tops(members, upper_trans, couplers, upper):
    position = lax.axis_index(BRANCH)
    rank = upper_trans.shape[1]
    height = members.bit_length() - 1
    blank = jnp.zeros((rank, LANES - rank), F32)

    def place(group, value):
        upper[0, group], upper[1, group] = split(value)

    def transfer(index, c):
        return upper_trans[index * 2 + c]

    def child(j):
        mixer = members - (members >> (j - 1)) + (position >> j)
        return transfer(mixer, (position >> (j - 1)) & 1)

    paths = [None, child(1)]
    current = [[(position ^ 1, couplers[0])]] + [None] * (height - 1)
    left_to_do = list(range(height))
    while any(left_to_do[1:]) or any(entry is None for entry in current):
        for j in range(1, height):
            if current[j] is not None and left_to_do[j] > 0:
                lower = left_to_do[j]
                offset = members - (members >> (lower - 1))
                following = []
                for index, matrix in current[j]:
                    for c in range(2):
                        mixed = product(matrix, transfer(offset + index, c), contract_nn)
                        following.append((2 * index + c, mixed))
                current[j] = following
                left_to_do[j] = lower - 1
        for j in range(1, min(len(paths), height)):
            if current[j] is None:
                current[j] = [((position >> j) ^ 1, product(paths[j], couplers[j], contract_tn))]
        if len(paths) < height:
            paths.append(product(child(len(paths)), paths[-1], contract_nn))
        yield
    own = jnp.zeros((rank, LANES), F32)
    for j in range(height):
        if j < 2:
            for index, matrix in current[j]:
                wide = jnp.concatenate([matrix, blank], axis=1)
                own = own + pltpu.roll(wide, (index & 3) * rank, 1)
        else:
            for k in range(0, len(current[j]), 4):
                wide = jnp.concatenate([matrix for _, matrix in current[j][k : k + 4]], axis=1)
                place(current[j][k][0] >> 2, wide)
    place(position >> 2, own)


def near_half(
    first,
    halo_half,
    vec_far,
    near_src_far,
    near_count_far,
    near_mat_far,
    near,
    vec,
    near_src,
    near_count,
    near_mat,
    values,
    semaphores,
    block_semaphores,
    ahead,
    before,
):
    position = lax.axis_index(BRANCH)
    leaves, near_slots, leaf_size, _ = near_mat.shape
    leaf_dev = near_src.shape[1]
    vecs = vec.shape[0]
    halo = leaf_dev // 2
    upper = (position & 1) ^ (1 if first else 0)
    base = upper * halo
    skip = 0 if first else ahead.shape[0]
    arriving = fetch((vec_far, near_src_far, near_count_far), (vec, near_src, near_count), semaphores)
    sizes = ((leaves + 3) // 4 * 2, leaves - (leaves + 3) // 4 * 2)

    def chunk_copy(k):
        start = k * sizes[0]
        there = near_mat_far.at[pl.ds(base + skip + start, sizes[k])]
        return pltpu.make_async_copy(there, near_mat.at[pl.ds(start, sizes[k])], block_semaphores.at[k])

    for k in range(2):
        chunk_copy(k).start()
    if first:
        others = near_mat_far.at[pl.ds(halo - base, ahead.shape[0])]
        ahead_copy = pltpu.make_async_copy(others, ahead, semaphores.at[len(arriving)])
        ahead_copy.start()
    before()
    for copy in arriving:
        copy.wait()
    left = lane_part(vecs, leaf_size) == 0

    def lay(base, block):
        for m in range(block.shape[1] // LANES):
            pair = block[:, m * LANES : (m + 1) * LANES]
            swapped = pltpu.roll(pair, leaf_size, 1)
            for c, twice in enumerate((jnp.where(left, pair, swapped), jnp.where(left, swapped, pair))):
                high, low = split(twice)
                values[base + 2 * m + c, :vecs] = high
                values[base + 2 * m + c, vecs:] = low

    lay(upper * (halo + leaf_dev), halo_half[...])
    lay(halo, vec[...])
    values[2 * leaf_dev] = jnp.zeros((2 * vecs, LANES), BF16)
    shift = halo - position * leaf_dev
    wide_left = lane_part(2 * vecs, leaf_size) == 0

    def source(leaf, slot):
        live = slot < near_count[0, base + leaf]
        return values[jnp.where(live, near_src[slot, base + leaf] + shift, 2 * leaf_dev)]

    def two_leaves(pair, blocks, start):
        total = None
        leaves = (2 * pair, 2 * pair + 1)
        for tile in range(0, near_slots, 4):
            columns = min(4, near_slots - tile)
            rows_x = []
            rows_w = []
            for leaf in leaves:
                xs = []
                ws = []
                for i in range(tile, tile + columns, 2):
                    if i + 1 < tile + columns:
                        xs.append(jnp.where(wide_left, source(leaf, i), source(leaf, i + 1)))
                        two = [blocks[leaf - start, i], blocks[leaf - start, i + 1]]
                        ws.append(jnp.concatenate(two, axis=1))
                    else:
                        xs.append(source(leaf, i))
                        blank = jnp.zeros((leaf_size, LANES - leaf_size), F32)
                        ws.append(jnp.concatenate([blocks[leaf - start, i], blank], axis=1))
                rows_x.append(jnp.concatenate(xs, axis=1) if len(xs) > 1 else xs[0])
                rows_w.append(jnp.concatenate(ws, axis=1) if len(ws) > 1 else ws[0])
            x = jnp.concatenate(rows_x, axis=0)
            high, low = split(jnp.concatenate(rows_w, axis=0))
            term = contract_nt(x, high) + contract_nt(x, low)
            total = term if total is None else total + term
        first = total[:vecs] + total[vecs : 2 * vecs]
        second = total[2 * vecs : 3 * vecs] + total[3 * vecs :]
        lanes = pl.ds(pl.multiple_of((base // 2 + pair) * LANES, LANES), LANES)
        near[:, lanes] = jnp.where(left, first, second)

    for pair in range(skip // 2):
        two_leaves(pair, ahead, 0)
    for k in range(2):
        chunk_copy(k).wait()
        for m in range(sizes[k] // 2):
            two_leaves((skip + k * sizes[0]) // 2 + m, near_mat, skip)
    if first:
        ahead_copy.wait()


def first_kernel(
    members,
    slots,
    halo_half,
    vec_far,
    near_src_far,
    near_count_far,
    near_mat_far,
    coup_mat_far,
    coup_tgt_far,
    near,
    coup,
    targets,
    ahead,
    coup_mat,
    coup_semaphores,
    *scratch,
):
    arriving = fetch((coup_mat_far, coup_tgt_far), (coup_mat, targets), coup_semaphores)

    def before():
        for copy in arriving:
            copy.wait()
        pack_couplings(members, slots, coup_mat, coup)

    near_half(True, halo_half, vec_far, near_src_far, near_count_far, near_mat_far, near, *scratch, ahead, before)


def second_kernel(
    halo_half, vec_far, near_src_far, near_count_far, near_mat_far, near_first, ahead, near, *scratch
):
    del near_first
    inputs = (halo_half, vec_far, near_src_far, near_count_far, near_mat_far)
    near_half(False, *inputs, near, *scratch, ahead, lambda: None)


def down_kernel(
    members,
    slots,
    incoming,
    coup,
    upper,
    weights,
    near,
    targets,
    out,
    coup_tgt,
    parts_far,
    pieces,
    semaphores,
):
    arriving = fetch((targets,), (coup_tgt,), semaphores)
    basis_high, basis_low, trans_high, trans_low = (weights.at[i] for i in range(4))
    vecs = out.shape[0]
    rank = LANES // slots
    groups = parts_far.shape[1]
    parts_far[...] = jnp.zeros(parts_far.shape, F32)
    part = lane_part(vecs, rank)

    blank = jnp.zeros((slots * vecs, LANES - rank), F32)

    def couple(source):
        values = incoming[source, :vecs]
        rows = jnp.concatenate([jnp.where(part == j, values, 0.0) for j in range(slots)], axis=0)
        narrow = times(rows, coup[0, source], coup[1, source], contract_nt)
        pieces[source] = jnp.concatenate([narrow, blank], axis=1)

    over(members, couple)

    few = lane_part(vecs // 2, rank)
    term = jnp.zeros((vecs, rank), F32)
    for g in range(members // 4):
        first = jnp.zeros((vecs // 2, LANES), F32)
        second = jnp.zeros((vecs // 2, LANES), F32)
        for q in range(4):
            rows = incoming[4 * g + q, vecs:]
            first = jnp.where(few == q, rows, first)
            second = jnp.where(few == (q + 1) % 4, rows, second)
        tops = jnp.concatenate([first, pltpu.roll(second, LANES - rank, 1)], axis=0)
        term = term + times(tops, upper[0, g], upper[1, g], contract_nt)
    sides = [jnp.zeros((vecs, 2 * rank), F32), term, jnp.zeros((vecs, rank), F32)]
    term = jnp.concatenate(sides, axis=1)
    arriving[0].wait()

    def scatter(source):
        for j in range(slots):
            node = coup_tgt[j, source]
            alone = pieces[source, j * vecs : (j + 1) * vecs]
            parts_far[j, node >> 2] += pltpu.roll(alone, (node & 3) * rank, 1)

    over(members, scatter)
    far = [sum(parts_far[j, g] for j in range(1, slots)) + parts_far[0, g] for g in range(groups)]

    left = part < 2
    weight = trans_high.shape[0] - 1

    def first_half(x):
        return jnp.where(left, x, 0.0)

    def second_half(x):
        return jnp.where(left, 0.0, x)

    def spread(x, high, low):
        both = times(jnp.concatenate([first_half(x), second_half(x)], axis=0), high, low, contract_nn)
        return both[:vecs], both[vecs:]

    first = groups - 2
    high, low = trans_high[weight], trans_low[weight]
    base = far[first + 1] + term
    two = base + times(second_half(base), high, low, contract_nn)
    level = [far[first] + times(first_half(two), high, low, contract_nn)]
    while first > 0:
        first -= 2 * len(level)
        weight -= len(level)
        children = []
        for g, value in enumerate(level):
            pair = spread(value, trans_high[weight + g], trans_low[weight + g])
            children.append(far[first + 2 * g] + pair[0])
            children.append(far[first + 2 * g + 1] + pair[1])
        level = children
    for g, value in enumerate(level):
        for c, points in enumerate(spread(value, basis_high[g], basis_low[g])):
            lanes = slice(LANES * (2 * g + c), LANES * (2 * g + c + 1))
            out[:, lanes] = near[:, lanes] + points


def in_hbm(x):
    return pltpu.with_memory_space_constraint(x, pltpu.HBM)


HBM_SPEC = pl.BlockSpec(memory_space=pltpu.HBM)
VMEM_SPEC = pl.BlockSpec(memory_space=pltpu.VMEM)


def params(mib):
    return pltpu.CompilerParams(vmem_limit_bytes=mib * MIB)


def cost(flops, size):
    return pl.CostEstimate(flops=flops, bytes_accessed=size, transcendentals=0)


def body(
    vectors,
    basis,
    trans,
    upper_trans,
    upper_coup,
    send_node,
    send_count,
    coup_tgt,
    coup_mat,
    near_src,
    near_count,
    near_mat,
):
    vecs, points = vectors.shape
    leaf_dev, rank, leaf_size = basis.shape
    members = lax.axis_size(BRANCH)
    slots = send_node.shape[2]
    groups = leaf_dev // 4
    node_groups = 2 * groups
    trans_blocks = trans.reshape(-1, rank, rank)
    coup_blocks = coup_mat.reshape(-1, rank, rank)
    upper_blocks = upper_trans.reshape(-1, rank, rank)
    shape = jax.ShapeDtypeStruct

    def held(*dims):
        return shape(dims, BF16)

    height = members.bit_length() - 1
    outgoing, sub_half, cross_half, weights, upper = pl.pallas_call(
        functools.partial(up_kernel, members, slots),
        out_shape=[
            shape((members, vecs + vecs // 2, LANES), F32),
            shape((vecs, points // 2), F32),
            shape((vecs, points // 2), F32),
            held(4, groups, LANES, LANES),
            held(2, members // 4, rank, LANES),
        ],
        in_specs=[HBM_SPEC] * 7,
        out_specs=[VMEM_SPEC] * 5,
        scratch_shapes=[
            pltpu.VMEM(upper_blocks.shape, F32),
            pltpu.VMEM((height, rank, rank), F32),
            pltpu.VMEM((vecs, points), F32),
            pltpu.VMEM(basis.shape, F32),
            pltpu.VMEM(trans_blocks.shape, F32),
            pltpu.SMEM((slots, members), jnp.int32),
            pltpu.SMEM((1, members), jnp.int32),
            pltpu.VMEM((4 * node_groups + 8, vecs, LANES), F32),
            pltpu.SemaphoreType.DMA((7,)),
            pltpu.SemaphoreType.DMA((1 + height,)),
        ],
        compiler_params=params(8 + members // 4),
        name="up",
    )(
        in_hbm(vectors),
        in_hbm(basis),
        in_hbm(trans_blocks),
        in_hbm(jnp.transpose(send_node[0])),
        in_hbm(send_count),
        in_hbm(upper_blocks),
        in_hbm(upper_coup),
    )
    incoming = lax.all_to_all(outgoing, BRANCH, split_axis=0, concat_axis=0, tiled=True)
    sub_got = lax.ppermute(sub_half, BRANCH, [(i, i ^ 1) for i in range(members)])
    pairs = [(i, i + 1) for i in range(1, members - 1, 2)]
    cross_got = lax.ppermute(cross_half, BRANCH, pairs + [(b, a) for a, b in pairs])

    def near_scratch(leaves):
        return [
            pltpu.VMEM((vecs, points), F32),
            pltpu.SMEM(near_src.shape[::-1], jnp.int32),
            pltpu.SMEM((1, leaf_dev), jnp.int32),
            pltpu.VMEM((leaves,) + near_mat.shape[1:], F32),
            pltpu.VMEM((2 * leaf_dev + 1, 2 * vecs, LANES), BF16),
            pltpu.SemaphoreType.DMA((4,)),
            pltpu.SemaphoreType.DMA((2,)),
        ]

    ahead_leaves = AHEAD
    near_inputs = (
        in_hbm(vectors),
        in_hbm(jnp.transpose(near_src)),
        in_hbm(near_count.reshape(1, -1)),
        in_hbm(near_mat),
    )
    near, coup, targets, ahead = pl.pallas_call(
        functools.partial(first_kernel, members, slots),
        out_shape=[
            shape((vecs, points), F32),
            held(2, members, rank, LANES),
            shape((slots, members), jnp.int32),
            shape((ahead_leaves,) + near_mat.shape[1:], F32),
        ],
        in_specs=[VMEM_SPEC] + [HBM_SPEC] * 6,
        out_specs=[VMEM_SPEC] * 4,
        scratch_shapes=[
            pltpu.VMEM(coup_blocks.shape, F32),
            pltpu.SemaphoreType.DMA((2,)),
        ]
        + near_scratch(leaf_dev // 2),
        compiler_params=params(12 + members // 4),
        cost_estimate=cost(1 << 28, 16 << 20),
        name="near_first",
    )(
        sub_got,
        *near_inputs,
        in_hbm(coup_blocks),
        in_hbm(jnp.transpose(coup_tgt[0])),
    )

    near = pl.pallas_call(
        second_kernel,
        out_shape=shape((vecs, points), F32),
        in_specs=[VMEM_SPEC] + [HBM_SPEC] * 4 + [VMEM_SPEC] * 2,
        out_specs=VMEM_SPEC,
        scratch_shapes=near_scratch(leaf_dev // 2 - ahead_leaves),
        input_output_aliases={5: 0},
        compiler_params=params(12 + members // 4),
        cost_estimate=cost(1 << 28, 8 << 20),
        name="near_second",
    )(cross_got, *near_inputs, near, ahead)

    return pl.pallas_call(
        functools.partial(down_kernel, members, slots),
        out_shape=shape((vecs, points), F32),
        in_specs=[VMEM_SPEC] * 6,
        out_specs=VMEM_SPEC,
        scratch_shapes=[
            pltpu.SMEM((slots, members), jnp.int32),
            pltpu.VMEM((slots, node_groups, vecs, LANES), F32),
            pltpu.VMEM((members, slots * vecs, LANES), F32),
            pltpu.SemaphoreType.DMA((1,)),
        ],
        compiler_params=params(8 + members // 4),
        name="down",
    )(
        incoming,
        coup,
        upper,
        weights,
        near,
        targets,
    )


def solution(mesh):
    spread = ("parts",) + BRANCH
    return jax.shard_map(
        body,
        mesh=mesh,
        in_specs=(
            P(None, spread),
            P(spread, None, None),
            P(spread, None, None, None, None),
            P("parts", None, None, None),
            P("parts", None, None),
            P(spread, None, None),
            P(spread, None),
            P(spread, None, None),
            P(spread, None, None, None, None),
            P(spread, None),
            P(spread),
            P(spread, None, None, None),
        ),
        out_specs=P(None, spread),
        check_vma=False,
    )
```

```python
import functools

import jax
import jax.numpy as jnp
from jax import lax
from jax.experimental import pallas as pl
from jax.experimental.pallas import tpu as pltpu
from jax.sharding import PartitionSpec as P

BRANCH = ("leaf", "sub")
LANES = 128
F32 = jnp.float32
BF16 = jnp.bfloat16
MIB = 1 << 20
AHEAD = 6


def split(x):
    high = x.astype(BF16)
    low = (x - high.astype(F32)).astype(BF16)
    return high, low


def contract_nt(a, b):
    return lax.dot_general(a, b, (((1,), (1,)), ((), ())), preferred_element_type=F32)


def contract_nn(a, b):
    return lax.dot_general(a, b, (((1,), (0,)), ((), ())), preferred_element_type=F32)


def contract_tn(a, b):
    return lax.dot_general(a, b, (((0,), (0,)), ((), ())), preferred_element_type=F32)


def times(x, high, low, dot):
    rows = x.shape[0]
    x_high, x_low = split(x)
    both = dot(jnp.concatenate([x_high, x_low], axis=0), high)
    return both[:rows] + both[rows:] + dot(x_high, low)


def product(a, b, dot):
    a_high, a_low = split(a)
    b_high, b_low = split(b)
    return dot(a_high, b_high) + (dot(a_high, b_low) + dot(a_low, b_high))


def lane_part(rows, part):
    return lax.broadcasted_iota(jnp.int32, (rows, LANES), 1) // part


def over(count, body, step=16):
    if count <= step:
        for i in range(count):
            body(i)
    else:

        def several(k, carry):
            for u in range(step):
                body(k * step + u)
            return carry

        lax.fori_loop(0, count // step, several, 0)


def fetch(sources, targets, semaphores):
    copies = []
    for i, (source, target) in enumerate(zip(sources, targets)):
        copies.append(pltpu.make_async_copy(source, target, semaphores.at[i]))
        copies[i].start()
    return copies


def up_kernel(
    members,
    slots,
    vec_far,
    basis_far,
    trans_far,
    send_node_far,
    send_count_far,
    upper_trans_far,
    upper_coup_far,
    outgoing,
    sub_half,
    cross_half,
    weights,
    upper,
    upper_trans,
    couplers,
    vec,
    basis,
    trans,
    send_node,
    send_count,
    rolled,
    semaphores,
    upper_semaphores,
):
    position = lax.axis_index(BRANCH)
    half = vec.shape[1] // 2
    start = (position & 1) * half
    at_partner = vec_far.at[:, pl.ds(pl.multiple_of(half - start, LANES), half)]
    at_neighbour = vec_far.at[:, pl.ds(pl.multiple_of(start, LANES), half)]
    wanted = fetch((vec_far, basis_far), (vec, basis), semaphores)
    sources = [upper_trans_far]
    targets = [upper_trans]
    for j in range(couplers.shape[0]):
        sources.append(upper_coup_far.at[2 * members - 2 * (members >> j) + (position >> j)])
        targets.append(couplers.at[j])
    upper_arriving = fetch(sources, targets, upper_semaphores)
    others = fetch(
        (trans_far, send_node_far, send_count_far, at_partner, at_neighbour),
        (trans, send_node, send_count, sub_half, cross_half),
        semaphores.at[pl.ds(2, 5)],
    )
    arriving = wanted + others
    basis_high, basis_low, trans_high, trans_low = (weights.at[i] for i in range(4))
    leaf_dev, rank, leaf_size = basis.shape
    vecs = vec.shape[0]
    left = lane_part(vecs, LANES // 2) == 0
    blank = jnp.zeros((rank, LANES // 2), F32)

    arriving[0].wait()
    arriving[1].wait()
    for leaf in range(leaf_dev):
        group, q = leaf // 4, leaf % 4
        high, low = split(jnp.concatenate([basis[leaf], blank] if q % 2 == 0 else [blank, basis[leaf]], axis=1))
        basis_high[group, q * rank : (q + 1) * rank] = high
        basis_low[group, q * rank : (q + 1) * rank] = low
    def keep(group, value):
        for k in range(4):
            rolled[4 * group + k] = value if k == 0 else pltpu.roll(value, k * rank, 1)

    def joined(first, second, high, low):
        both = times(jnp.concatenate([first, second], axis=0), high, low, contract_nt)
        return jnp.where(left, both[:vecs], both[vecs:])

    level = []
    for g in range(leaf_dev // 4):
        first = vec[:, 2 * LANES * g : 2 * LANES * g + LANES]
        second = vec[:, 2 * LANES * g + LANES : 2 * LANES * (g + 1)]
        level.append(joined(first, second, basis_high[g], basis_low[g]))
        keep(g, level[g])
    arriving[2].wait()
    for copy in upper_arriving:
        copy.wait()
    arriving[3].wait()
    arriving[4].wait()
    tops = map_tops(members, upper_trans, couplers, upper)
    for node in range(leaf_dev):
        group, q = node // 4, node % 4
        if node < leaf_dev - 1:
            pair = [trans[2 * node], trans[2 * node + 1]]
            high, low = split(jnp.concatenate(pair + [blank] if q % 2 == 0 else [blank] + pair, axis=1))
        else:
            high = low = jnp.zeros((rank, LANES), BF16)
        trans_high[group, q * rank : (q + 1) * rank] = high
        trans_low[group, q * rank : (q + 1) * rank] = low
    done = leaf_dev // 4
    weight = 0
    while len(level) > 1:
        nodes = []
        next(tops, None)
        for g in range(len(level) // 2):
            nodes.append(joined(level[2 * g], level[2 * g + 1], trans_high[weight], trans_low[weight]))
            keep(done, nodes[g])
            weight += 1
            done += 1
        level = nodes
    two = jnp.where(left, times(level[0], trans_high[weight], trans_low[weight], contract_nt), 0.0)
    next(tops, None)
    top = times(two, trans_high[weight], trans_low[weight], contract_nt)
    for _ in tops:
        pass
    keep(done, jnp.where(left, two, top))
    blank_index = 4 * (done + 1)
    rolled[blank_index] = jnp.zeros((vecs, LANES), F32)

    part = lane_part(vecs, rank)
    few = lane_part(vecs // 2, rank)
    first = position & 3
    second = (position + 1) & 3
    top_rows = jnp.where(
        few == first,
        rolled[4 * done + ((first - 2) & 3), : vecs // 2],
        jnp.where(few == second, rolled[4 * done + ((second - 2) & 3), vecs // 2 :], 0.0),
    )

    def pick(target):
        count = send_count[0, target]
        value = None
        for j in range(slots):
            node = send_node[j, target]
            index = (node >> 2) * 4 + ((j - node) & 3)
            piece = rolled[jnp.where(j < count, index, blank_index)]
            value = piece if value is None else jnp.where(part == j, piece, value)
        outgoing[target, :vecs] = value
        outgoing[target, vecs:] = top_rows

    over(members, pick)
    arriving[5].wait()
    arriving[6].wait()


def pack_couplings(members, slots, coup_mat, coup):
    def one(source):
        blocks = [coup_mat[source * slots + j] for j in range(slots)]
        coup[0, source], coup[1, source] = split(jnp.concatenate(blocks, axis=1))

    over(members, one)


def map_tops(members, upper_trans, couplers, upper):
    position = lax.axis_index(BRANCH)
    rank = upper_trans.shape[1]
    height = members.bit_length() - 1
    blank = jnp.zeros((rank, LANES - rank), F32)

    def place(group, value):
        upper[0, group], upper[1, group] = split(value)

    def transfer(index, c):
        return upper_trans[index * 2 + c]

    def child(j):
        mixer = members - (members >> (j - 1)) + (position >> j)
        return transfer(mixer, (position >> (j - 1)) & 1)

    paths = [None, child(1)]
    current = [[(position ^ 1, couplers[0])]] + [None] * (height - 1)
    left_to_do = list(range(height))
    while any(left_to_do[1:]) or any(entry is None for entry in current):
        for j in range(1, height):
            if current[j] is not None and left_to_do[j] > 0:
                lower = left_to_do[j]
                offset = members - (members >> (lower - 1))
                following = []
                for index, matrix in current[j]:
                    for c in range(2):
                        mixed = product(matrix, transfer(offset + index, c), contract_nn)
                        following.append((2 * index + c, mixed))
                current[j] = following
                left_to_do[j] = lower - 1
        for j in range(1, min(len(paths), height)):
            if current[j] is None:
                current[j] = [((position >> j) ^ 1, product(paths[j], couplers[j], contract_tn))]
        if len(paths) < height:
            paths.append(product(child(len(paths)), paths[-1], contract_nn))
        yield
    own = jnp.zeros((rank, LANES), F32)
    for j in range(height):
        if j < 2:
            for index, matrix in current[j]:
                wide = jnp.concatenate([matrix, blank], axis=1)
                own = own + pltpu.roll(wide, (index & 3) * rank, 1)
        else:
            for k in range(0, len(current[j]), 4):
                wide = jnp.concatenate([matrix for _, matrix in current[j][k : k + 4]], axis=1)
                place(current[j][k][0] >> 2, wide)
    place(position >> 2, own)


def near_half(
    first,
    halo_half,
    vec_far,
    near_src_far,
    near_count_far,
    near_mat_far,
    near,
    vec,
    near_src,
    near_count,
    near_mat,
    values,
    semaphores,
    block_semaphores,
    ahead,
    before,
):
    position = lax.axis_index(BRANCH)
    leaves, near_slots, leaf_size, _ = near_mat.shape
    leaf_dev = near_src.shape[1]
    vecs = vec.shape[0]
    halo = leaf_dev // 2
    upper = (position & 1) ^ (1 if first else 0)
    base = upper * halo
    skip = 0 if first else ahead.shape[0]
    arriving = fetch((vec_far, near_src_far, near_count_far), (vec, near_src, near_count), semaphores)
    sizes = ((leaves + 3) // 4 * 2, leaves - (leaves + 3) // 4 * 2)

    def chunk_copy(k):
        start = k * sizes[0]
        there = near_mat_far.at[pl.ds(base + skip + start, sizes[k])]
        return pltpu.make_async_copy(there, near_mat.at[pl.ds(start, sizes[k])], block_semaphores.at[k])

    for k in range(2):
        chunk_copy(k).start()
    if first:
        others = near_mat_far.at[pl.ds(halo - base, ahead.shape[0])]
        ahead_copy = pltpu.make_async_copy(others, ahead, semaphores.at[len(arriving)])
        ahead_copy.start()
    before()
    left = lane_part(vecs, leaf_size) == 0

    def lay(base, block):
        for m in range(block.shape[1] // LANES):
            pair = block[:, m * LANES : (m + 1) * LANES]
            swapped = pltpu.roll(pair, leaf_size, 1)
            for c, twice in enumerate((jnp.where(left, pair, swapped), jnp.where(left, swapped, pair))):
                high, low = split(twice)
                values[base + 2 * m + c, :vecs] = high
                values[base + 2 * m + c, vecs:] = low

    lay(upper * (halo + leaf_dev), halo_half[...])
    values[2 * leaf_dev] = jnp.zeros((2 * vecs, LANES), BF16)
    for copy in arriving:
        copy.wait()
    lay(halo, vec[...])
    shift = halo - position * leaf_dev
    wide_left = lane_part(2 * vecs, leaf_size) == 0

    def source(leaf, slot):
        live = slot < near_count[0, base + leaf]
        return values[jnp.where(live, near_src[slot, base + leaf] + shift, 2 * leaf_dev)]

    def two_leaves(pair, blocks, start):
        total = None
        leaves = (2 * pair, 2 * pair + 1)
        for tile in range(0, near_slots, 4):
            columns = min(4, near_slots - tile)
            rows_x = []
            rows_w = []
            for leaf in leaves:
                xs = []
                ws = []
                for i in range(tile, tile + columns, 2):
                    if i + 1 < tile + columns:
                        xs.append(jnp.where(wide_left, source(leaf, i), source(leaf, i + 1)))
                        two = [blocks[leaf - start, i], blocks[leaf - start, i + 1]]
                        ws.append(jnp.concatenate(two, axis=1))
                    else:
                        xs.append(source(leaf, i))
                        blank = jnp.zeros((leaf_size, LANES - leaf_size), F32)
                        ws.append(jnp.concatenate([blocks[leaf - start, i], blank], axis=1))
                rows_x.append(jnp.concatenate(xs, axis=1) if len(xs) > 1 else xs[0])
                rows_w.append(jnp.concatenate(ws, axis=1) if len(ws) > 1 else ws[0])
            x = jnp.concatenate(rows_x, axis=0)
            high, low = split(jnp.concatenate(rows_w, axis=0))
            term = contract_nt(x, high) + contract_nt(x, low)
            total = term if total is None else total + term
        first = total[:vecs] + total[vecs : 2 * vecs]
        second = total[2 * vecs : 3 * vecs] + total[3 * vecs :]
        lanes = pl.ds(pl.multiple_of((base // 2 + pair) * LANES, LANES), LANES)
        near[:, lanes] = jnp.where(left, first, second)

    for pair in range(skip // 2):
        two_leaves(pair, ahead, 0)
    for k in range(2):
        chunk_copy(k).wait()
        for m in range(sizes[k] // 2):
            two_leaves((skip + k * sizes[0]) // 2 + m, near_mat, skip)
    if first:
        ahead_copy.wait()


def first_kernel(
    members,
    slots,
    halo_half,
    vec_far,
    near_src_far,
    near_count_far,
    near_mat_far,
    coup_mat_far,
    coup_tgt_far,
    near,
    coup,
    targets,
    ahead,
    coup_mat,
    coup_semaphores,
    *scratch,
):
    arriving = fetch((coup_mat_far, coup_tgt_far), (coup_mat, targets), coup_semaphores)

    def before():
        for copy in arriving:
            copy.wait()
        pack_couplings(members, slots, coup_mat, coup)

    near_half(True, halo_half, vec_far, near_src_far, near_count_far, near_mat_far, near, *scratch, ahead, before)


def second_kernel(
    halo_half, vec_far, near_src_far, near_count_far, near_mat_far, near_first, ahead, near, *scratch
):
    del near_first
    inputs = (halo_half, vec_far, near_src_far, near_count_far, near_mat_far)
    near_half(False, *inputs, near, *scratch, ahead, lambda: None)


def down_kernel(
    members,
    slots,
    incoming,
    coup,
    upper,
    weights,
    near,
    targets,
    out,
    coup_tgt,
    parts_far,
    pieces,
    semaphores,
):
    arriving = fetch((targets,), (coup_tgt,), semaphores)
    basis_high, basis_low, trans_high, trans_low = (weights.at[i] for i in range(4))
    vecs = out.shape[0]
    rank = LANES // slots
    groups = parts_far.shape[1]
    parts_far[...] = jnp.zeros(parts_far.shape, F32)
    part = lane_part(vecs, rank)

    blank = jnp.zeros((slots * vecs, LANES - rank), F32)

    def couple(source):
        values = incoming[source, :vecs]
        rows = jnp.concatenate([jnp.where(part == j, values, 0.0) for j in range(slots)], axis=0)
        narrow = times(rows, coup[0, source], coup[1, source], contract_nt)
        pieces[source] = jnp.concatenate([narrow, blank], axis=1)

    over(members, couple)

    few = lane_part(vecs // 2, rank)
    term = jnp.zeros((vecs, rank), F32)
    for g in range(members // 4):
        first = jnp.zeros((vecs // 2, LANES), F32)
        second = jnp.zeros((vecs // 2, LANES), F32)
        for q in range(4):
            rows = incoming[4 * g + q, vecs:]
            first = jnp.where(few == q, rows, first)
            second = jnp.where(few == (q + 1) % 4, rows, second)
        tops = jnp.concatenate([first, pltpu.roll(second, LANES - rank, 1)], axis=0)
        term = term + times(tops, upper[0, g], upper[1, g], contract_nt)
    sides = [jnp.zeros((vecs, 2 * rank), F32), term, jnp.zeros((vecs, rank), F32)]
    term = jnp.concatenate(sides, axis=1)
    arriving[0].wait()

    def scatter(source):
        for j in range(slots):
            node = coup_tgt[j, source]
            alone = pieces[source, j * vecs : (j + 1) * vecs]
            parts_far[j, node >> 2] += pltpu.roll(alone, (node & 3) * rank, 1)

    over(members, scatter)
    far = [sum(parts_far[j, g] for j in range(1, slots)) + parts_far[0, g] for g in range(groups)]

    left = part < 2
    weight = trans_high.shape[0] - 1

    def first_half(x):
        return jnp.where(left, x, 0.0)

    def second_half(x):
        return jnp.where(left, 0.0, x)

    def spread(x, high, low):
        both = times(jnp.concatenate([first_half(x), second_half(x)], axis=0), high, low, contract_nn)
        return both[:vecs], both[vecs:]

    first = groups - 2
    high, low = trans_high[weight], trans_low[weight]
    base = far[first + 1] + term
    two = base + times(second_half(base), high, low, contract_nn)
    level = [far[first] + times(first_half(two), high, low, contract_nn)]
    while first > 0:
        first -= 2 * len(level)
        weight -= len(level)
        children = []
        for g, value in enumerate(level):
            pair = spread(value, trans_high[weight + g], trans_low[weight + g])
            children.append(far[first + 2 * g] + pair[0])
            children.append(far[first + 2 * g + 1] + pair[1])
        level = children
    for g, value in enumerate(level):
        for c, points in enumerate(spread(value, basis_high[g], basis_low[g])):
            lanes = slice(LANES * (2 * g + c), LANES * (2 * g + c + 1))
            out[:, lanes] = near[:, lanes] + points


def in_hbm(x):
    return pltpu.with_memory_space_constraint(x, pltpu.HBM)


HBM_SPEC = pl.BlockSpec(memory_space=pltpu.HBM)
VMEM_SPEC = pl.BlockSpec(memory_space=pltpu.VMEM)


def params(mib):
    return pltpu.CompilerParams(vmem_limit_bytes=mib * MIB)


def cost(flops, size):
    return pl.CostEstimate(flops=flops, bytes_accessed=size, transcendentals=0)


def body(
    vectors,
    basis,
    trans,
    upper_trans,
    upper_coup,
    send_node,
    send_count,
    coup_tgt,
    coup_mat,
    near_src,
    near_count,
    near_mat,
):
    vecs, points = vectors.shape
    leaf_dev, rank, leaf_size = basis.shape
    members = lax.axis_size(BRANCH)
    slots = send_node.shape[2]
    groups = leaf_dev // 4
    node_groups = 2 * groups
    trans_blocks = trans.reshape(-1, rank, rank)
    coup_blocks = coup_mat.reshape(-1, rank, rank)
    upper_blocks = upper_trans.reshape(-1, rank, rank)
    shape = jax.ShapeDtypeStruct

    def held(*dims):
        return shape(dims, BF16)

    height = members.bit_length() - 1
    outgoing, sub_half, cross_half, weights, upper = pl.pallas_call(
        functools.partial(up_kernel, members, slots),
        out_shape=[
            shape((members, vecs + vecs // 2, LANES), F32),
            shape((vecs, points // 2), F32),
            shape((vecs, points // 2), F32),
            held(4, groups, LANES, LANES),
            held(2, members // 4, rank, LANES),
        ],
        in_specs=[HBM_SPEC] * 7,
        out_specs=[VMEM_SPEC] * 5,
        scratch_shapes=[
            pltpu.VMEM(upper_blocks.shape, F32),
            pltpu.VMEM((height, rank, rank), F32),
            pltpu.VMEM((vecs, points), F32),
            pltpu.VMEM(basis.shape, F32),
            pltpu.VMEM(trans_blocks.shape, F32),
            pltpu.SMEM((slots, members), jnp.int32),
            pltpu.SMEM((1, members), jnp.int32),
            pltpu.VMEM((4 * node_groups + 8, vecs, LANES), F32),
            pltpu.SemaphoreType.DMA((7,)),
            pltpu.SemaphoreType.DMA((1 + height,)),
        ],
        compiler_params=params(8 + members // 4),
        name="up",
    )(
        in_hbm(vectors),
        in_hbm(basis),
        in_hbm(trans_blocks),
        in_hbm(jnp.transpose(send_node[0])),
        in_hbm(send_count),
        in_hbm(upper_blocks),
        in_hbm(upper_coup),
    )
    incoming = lax.all_to_all(outgoing, BRANCH, split_axis=0, concat_axis=0, tiled=True)
    sub_got = lax.ppermute(sub_half, BRANCH, [(i, i ^ 1) for i in range(members)])
    pairs = [(i, i + 1) for i in range(1, members - 1, 2)]
    cross_got = lax.ppermute(cross_half, BRANCH, pairs + [(b, a) for a, b in pairs])

    def near_scratch(leaves):
        return [
            pltpu.VMEM((vecs, points), F32),
            pltpu.SMEM(near_src.shape[::-1], jnp.int32),
            pltpu.SMEM((1, leaf_dev), jnp.int32),
            pltpu.VMEM((leaves,) + near_mat.shape[1:], F32),
            pltpu.VMEM((2 * leaf_dev + 1, 2 * vecs, LANES), BF16),
            pltpu.SemaphoreType.DMA((4,)),
            pltpu.SemaphoreType.DMA((2,)),
        ]

    ahead_leaves = AHEAD
    near_inputs = (
        in_hbm(vectors),
        in_hbm(jnp.transpose(near_src)),
        in_hbm(near_count.reshape(1, -1)),
        in_hbm(near_mat),
    )
    near, coup, targets, ahead = pl.pallas_call(
        functools.partial(first_kernel, members, slots),
        out_shape=[
            shape((vecs, points), F32),
            held(2, members, rank, LANES),
            shape((slots, members), jnp.int32),
            shape((ahead_leaves,) + near_mat.shape[1:], F32),
        ],
        in_specs=[VMEM_SPEC] + [HBM_SPEC] * 6,
        out_specs=[VMEM_SPEC] * 4,
        scratch_shapes=[
            pltpu.VMEM(coup_blocks.shape, F32),
            pltpu.SemaphoreType.DMA((2,)),
        ]
        + near_scratch(leaf_dev // 2),
        compiler_params=params(12 + members // 4),
        cost_estimate=cost(1 << 28, 16 << 20),
        name="near_first",
    )(
        sub_got,
        *near_inputs,
        in_hbm(coup_blocks),
        in_hbm(jnp.transpose(coup_tgt[0])),
    )

    near = pl.pallas_call(
        second_kernel,
        out_shape=shape((vecs, points), F32),
        in_specs=[VMEM_SPEC] + [HBM_SPEC] * 4 + [VMEM_SPEC] * 2,
        out_specs=VMEM_SPEC,
        scratch_shapes=near_scratch(leaf_dev // 2 - ahead_leaves),
        input_output_aliases={5: 0},
        compiler_params=params(12 + members // 4),
        cost_estimate=cost(1 << 28, 8 << 20),
        name="near_second",
    )(cross_got, *near_inputs, near, ahead)

    return pl.pallas_call(
        functools.partial(down_kernel, members, slots),
        out_shape=shape((vecs, points), F32),
        in_specs=[VMEM_SPEC] * 6,
        out_specs=VMEM_SPEC,
        scratch_shapes=[
            pltpu.SMEM((slots, members), jnp.int32),
            pltpu.VMEM((slots, node_groups, vecs, LANES), F32),
            pltpu.VMEM((members, slots * vecs, LANES), F32),
            pltpu.SemaphoreType.DMA((1,)),
        ],
        compiler_params=params(8 + members // 4),
        name="down",
    )(
        incoming,
        coup,
        upper,
        weights,
        near,
        targets,
    )


def solution(mesh):
    spread = ("parts",) + BRANCH
    return jax.shard_map(
        body,
        mesh=mesh,
        in_specs=(
            P(None, spread),
            P(spread, None, None),
            P(spread, None, None, None, None),
            P("parts", None, None, None),
            P("parts", None, None),
            P(spread, None, None),
            P(spread, None),
            P(spread, None, None),
            P(spread, None, None, None, None),
            P(spread, None),
            P(spread),
            P(spread, None, None, None),
        ),
        out_specs=P(None, spread),
        check_vma=False,
    )
```
